256 devices in a mesh: angle: 4 (over y_lo, core), slab: 64 (over x, z, y_hi).
Axes of the slice: x: 4, y: 4 (y_hi: 2, y_lo: 2; y = y_hi * 2 + y_lo), z: 8, core: 2. Of those that a mesh axis runs over, the one named last changes fastest.
Arguments:
- coefficients: float32 [45, 128, 32, 128], P(None, 'slab'), may hold values from -6 to 6
- harmonics: float32 [8, 8, 45], P('angle'), may hold values from -0.875 to 0.875
- stretch: float32 [8], P('angle'), may hold values from 0.5 to 0.75
- measured: float32 [8, 8, 16384], P('angle', None, 'slab'), may hold values from -24 to 24
- tile_pixel: int32 [8, 12288], P('angle', 'slab'), may hold values from 0 to 127
- tile_voxel: int32 [8, 12288], P('angle', 'slab'), may hold values from 0 to 63
- tile_shift: float32 [8, 12288], P('angle', 'slab'), may hold values from 0 to 32
- tile_count: int32 [8, 64], P('angle', 'slab'), may hold values from 96 to 192, as said below
Outputs:
- updated: float32 [45, 128, 32, 128], P(None, 'slab')
- misfit: float32 [8, 8, 16384], P('angle', None, 'slab')
The draws below stay inside these ranges and needn't reach their ends.
Inputs may be any that keep to these rules, and one draw needn't show every extreme that they name: `tile_voxel`: tile slots of slab d read voxel rows of slab d only. `tile_count`: every rotation has a slab with all 192 slots valid.
All inputs are finite; a program needn't handle non-finite values.
Results may differ from the reference program's by a relative error of at most 0.0001.
Values sent between devices are 32-bit elements; how exact they have to be, the bound alone decides.
A program may use at most 64 MiB of HBM per device.

```python
from functools import partial
import jax
import jax.numpy as jnp
from jax import lax

K = 45
SEG = 8
NX = 128
NY = 32
SZ = 2
PIX = 16384
ITERS = 2
TILES = 192
PTILES = 128
ROT = 8
NZ = 128
TILES_ALL = 12288
N_SLAB = 64


def draw_tile_count(key, part):
    key = jax.random.fold_in(key, 7)
    first, second = jax.random.split(key)
    counts = jax.random.randint(first, (ROT, N_SLAB), TILES // 2, TILES + 1)
    fullest = jax.random.randint(second, (ROT, 1), 0, N_SLAB)
    return jnp.where(jnp.arange(N_SLAB)[None, :] == fullest, TILES, counts).astype(jnp.int32)


def plant(entries, own_key, low, high):
    longest = entries.shape.index(max(entries.shape))
    spots = []
    for shift in (0, 1):
        where = [jax.random.randint(jax.random.fold_in(own_key, axis), (), 0, length) for axis, length in enumerate(entries.shape)]
        where[longest] = (where[longest] + shift) % entries.shape[longest]
        spots.append(tuple(where))
    return entries.at[spots[0]].set(low).at[spots[1]].set(high)


def levels(own_key, dims, cuts, least, top_value):
    level = 1.0
    for axis_at, parts in cuts:
        draws = jax.random.uniform(jax.random.fold_in(jax.random.fold_in(own_key, 6), axis_at), (parts,), jnp.float32, least / len(cuts), top_value / len(cuts))
        level = level * jnp.repeat(jnp.exp(draws), dims[axis_at] // parts).reshape((-1,) + (1,) * (len(dims) - 1 - axis_at))
    return level


def scatter_about(stream_key, shape, scale, most, cuts=(), kind=jnp.bfloat16):
    factor_of = levels(stream_key, shape, cuts, -0.22, 0.18) if cuts else 1.0
    array = jax.random.normal(stream_key, shape, jnp.float32) * scale * factor_of
    return jnp.minimum(jnp.maximum(array, -most), most).astype(kind)


def setup_inputs(seed: int = 0) -> dict:
    splits = jax.random.split(jax.random.key(seed), 9)
    coefficients = scatter_about(splits[0], (K, NZ, NY, NX), 1.0, 6.0, ((1, 64),), jnp.float32)
    harmonics = scatter_about(splits[1], (ROT, SEG, K), K ** -0.5, 0.875, ((0, 4),), jnp.float32)
    stretch = jnp.clip(0.5 + 0.25 * jax.random.uniform(splits[2], (ROT,), jnp.float32) ** levels(splits[2], (ROT,), ((0, 4),), -0.2, 0.2), 0.5, 0.75)
    measured = scatter_about(splits[3], (ROT, SEG, PIX), 4.0, 24.0, ((0, 4), (2, 64)), jnp.float32)
    tile_pixel = plant(jax.random.randint(splits[4], (ROT, TILES_ALL), 0, PTILES), jax.random.fold_in(splits[4], 1), 0, PTILES - 1).astype(jnp.int32)
    tile_voxel = plant(jax.random.randint(splits[5], (ROT, TILES_ALL), 0, SZ * NY), jax.random.fold_in(splits[5], 1), 0, (SZ * NY) - 1).astype(jnp.int32)
    tile_shift = jnp.clip(32.0 * jax.random.uniform(splits[6], (ROT, TILES_ALL), jnp.float32) ** levels(splits[6], (ROT, TILES_ALL), ((0, 4), (1, 64)), -0.2, 0.2), 0.0, 32.0)
    tile_count = draw_tile_count(jax.random.fold_in(splits[8], 71), 0)
    return dict(coefficients=coefficients, harmonics=harmonics, stretch=stretch, measured=measured, tile_pixel=tile_pixel, tile_voxel=tile_voxel, tile_shift=tile_shift, tile_count=tile_count)


tile_blocks = 4
step_size = 0.003
smoothing = 6.0


def footprint(shifts, stretch_value, width):
    position = jnp.arange(width).astype(shifts.dtype)
    offset = position[None, None, :] - shifts[:, None, None] - stretch_value * position[None, :, None]
    return jnp.maximum(0.0, 1.0 - jnp.abs(offset))


def project_rotation(seg_field, pixel_index, voxel_index, shifts, validity, stretch_value, pixel_tiles):
    segments, voxel_rows, width = seg_field.shape
    per_block = shifts.shape[0] // tile_blocks

    def accumulate(total, inputs_block):
        block_pixels, block_voxels, block_shifts, block_valid = inputs_block
        weights = footprint(block_shifts, stretch_value, width) * block_valid[:, None, None]
        picked = seg_field[:, block_voxels, :]
        contrib = jnp.einsum("stv,tvp->tsp", picked, weights, precision=lax.Precision.HIGHEST)
        return total.at[block_pixels].add(contrib), None

    inputs_all = tuple(entry.reshape(tile_blocks, per_block) for entry in (pixel_index, voxel_index, shifts, validity))
    total, unused = lax.scan(accumulate, jnp.zeros((pixel_tiles, segments, width), seg_field.dtype), inputs_all)
    return total.transpose(1, 0, 2).reshape(segments, pixel_tiles * width)


def back_rotation(misfit_rows, pixel_index, voxel_index, shifts, validity, stretch_value, voxel_rows):
    segments, pixel_tiles, width = misfit_rows.shape
    per_block = shifts.shape[0] // tile_blocks

    def accumulate(total, inputs_block):
        block_pixels, block_voxels, block_shifts, block_valid = inputs_block
        weights = footprint(block_shifts, stretch_value, width) * block_valid[:, None, None]
        picked = misfit_rows[:, block_pixels, :]
        contrib = jnp.einsum("stp,tvp->tsv", picked, weights, precision=lax.Precision.HIGHEST)
        return total.at[block_voxels].add(contrib), None

    inputs_all = tuple(entry.reshape(tile_blocks, per_block) for entry in (pixel_index, voxel_index, shifts, validity))
    total, unused = lax.scan(accumulate, jnp.zeros((voxel_rows, segments, width), misfit_rows.dtype), inputs_all)
    return total.transpose(1, 0, 2)


def yx_neighbours(field):
    padded = jnp.pad(field, ((0, 0), (0, 0), (1, 1), (1, 1)))
    return padded[:, :, 2:, 1:-1] + padded[:, :, :-2, 1:-1] + padded[:, :, 1:-1, 2:] + padded[:, :, 1:-1, :-2]


def slab_project(stretch_value, pixel_tiles, total, inputs_slab):
    field, pixel_index, voxel_index, shifts, validity = inputs_slab
    return total + project_rotation(field, pixel_index, voxel_index, shifts, validity, stretch_value, pixel_tiles), None


def slab_back(misfit_rows, stretch_value, voxel_rows, inputs_slab):
    pixel_index, voxel_index, shifts, validity = inputs_slab
    return back_rotation(misfit_rows, pixel_index, voxel_index, shifts, validity, stretch_value, voxel_rows)


def reference(coefficients, harmonics, stretch, measured, tile_pixel, tile_voxel, tile_shift, tile_count):
    channels, depth, height, width = coefficients.shape
    slabs = N_SLAB
    voxel_rows = depth // slabs * height
    rotations, segments, pixels = measured.shape
    pixel_tiles = pixels // width
    pixel_index = tile_pixel.reshape(rotations, slabs, TILES)
    voxel_index = tile_voxel.reshape(rotations, slabs, TILES)
    shift_all = tile_shift.reshape(rotations, slabs, TILES)
    validity = (jnp.arange(TILES)[None, None, :] < tile_count[:, :, None]).astype(tile_shift.dtype)
    coeffs = coefficients
    misfit = measured
    for iteration in range(ITERS):
        padded = jnp.pad(coeffs, ((0, 0), (1, 1), (0, 0), (0, 0)))
        laplace = 6.0 * coeffs - padded[:, 2:] - padded[:, :-2] - yx_neighbours(coeffs)
        flat = coeffs.reshape(channels, slabs, voxel_rows, width)
        misfits = []
        for rotation in range(rotations):
            seg_all = jnp.einsum("sk,kdqx->dsqx", harmonics[rotation], flat, precision=lax.Precision.HIGHEST)
            total, unused = lax.scan(partial(slab_project, stretch[rotation], pixel_tiles),
                                     jnp.zeros((segments, pixels), coeffs.dtype),
                                     (seg_all, pixel_index[rotation], voxel_index[rotation], shift_all[rotation], validity[rotation]))
            misfits.append(total - measured[rotation])
        misfit = jnp.stack(misfits)
        gradient = jnp.zeros((channels, slabs, voxel_rows, width), coeffs.dtype)
        for rotation in range(rotations):
            misfit_rows = misfit[rotation].reshape(segments, pixel_tiles, width)
            back_all = lax.map(partial(slab_back, misfit_rows, stretch[rotation], voxel_rows),
                               (pixel_index[rotation], voxel_index[rotation], shift_all[rotation], validity[rotation]))
            gradient = gradient + jnp.einsum("sk,dsqx->kdqx", harmonics[rotation], back_all, precision=lax.Precision.HIGHEST)
        coeffs = coeffs - step_size * (gradient.reshape(coeffs.shape) + smoothing * laplace)
    return coeffs, misfit
```

```python
import jax
import jax.numpy as jnp
from jax import lax
from jax.experimental import pallas as pl
from jax.experimental.pallas import tpu as pltpu
from jax.sharding import PartitionSpec as P

f32 = jnp.float32
MESH = pl.DeviceIdType.MESH
STEP = 0.003
SMOOTH = 6.0
NA = 2
FAR = 1.0e6

VM = pl.BlockSpec(memory_space=pltpu.VMEM)
SM = pl.BlockSpec(memory_space=pltpu.SMEM)
LIMIT = 48 * 2**20


def position():
    angle = lax.axis_index("angle")
    slab = lax.axis_index("slab")
    return angle, lax.div(slab, 16), lax.rem(lax.div(slab, 2), 8), lax.rem(slab, 2)


def device(angle, x, z, half):
    return (angle, (x * 8 + z) * 2 + half)


def greet(partners):
    barrier = pltpu.get_barrier_semaphore()
    for partner in partners:
        pl.semaphore_signal(barrier, inc=1, device_id=partner, device_id_type=MESH)
    pl.semaphore_wait(barrier, len(partners))


def send(src, dst, send_sem, recv_sem, target):
    copy = pltpu.make_async_remote_copy(
        src_ref=src, dst_ref=dst, send_sem=send_sem, recv_sem=recv_sem, device_id=target, device_id_type=MESH
    )
    copy.start()
    return copy


def dot(a, b):
    return jnp.dot(a, b, preferred_element_type=f32, precision=lax.Precision.HIGHEST)


def begin_kernel(c_ref, harm_ref, pack_ref, meas_ref, field_ref, harm_all_ref, pack_got, meas_got, out_ref, send_sem, recv_sem):
    angle, x, z, half = position()
    other = 1 - half
    partner = device(angle, x, z, other)
    peers = [device(lax.rem(angle + k, 4), x, z, half) for k in range(1, 4)]
    greet([partner] + peers)
    copies = [
        send(pack_ref, pack_got, send_sem.at[0], recv_sem.at[0], partner),
        send(meas_ref, meas_got, send_sem.at[1], recv_sem.at[1], partner),
    ]
    for k, peer in enumerate(peers):
        copies.append(send(harm_ref, harm_all_ref.at[angle], send_sem.at[2 + k], recv_sem.at[2 + k], peer))
    harm_all_ref[angle] = harm_ref[...]

    def fields(which, dest, base):
        rows = harm_ref[pl.ds(pl.multiple_of(which * 8, 8), 8), :][:, :48]
        for chunk in range(4):
            out = dot(rows, c_ref[chunk])
            for row in range(16):
                dest[base + chunk * 16 + row] = out[:, row * 128 : row * 128 + 128]

    fields(other, out_ref, 0)
    copies.append(send(out_ref, field_ref.at[pl.ds(64, 64)], send_sem.at[5], recv_sem.at[5], partner))
    fields(half, field_ref, 0)
    for copy in copies:
        copy.wait()


def begin(c_all, harm, pack, measured):
    return pl.pallas_call(
        begin_kernel,
        out_shape=(
            jax.ShapeDtypeStruct((128, 8, 128), f32),
            jax.ShapeDtypeStruct((4, 16, 128), f32),
            jax.ShapeDtypeStruct(pack.shape, f32),
            jax.ShapeDtypeStruct(measured.shape, f32),
        ),
        in_specs=[VM] * 4,
        out_specs=(VM,) * 4,
        scratch_shapes=[pltpu.VMEM((64, 8, 128), f32), pltpu.SemaphoreType.DMA((6,)), pltpu.SemaphoreType.DMA((6,))],
        compiler_params=pltpu.CompilerParams(collective_id=0, has_side_effects=True, vmem_limit_bytes=LIMIT),
        name="begin",
    )(c_all, harm, pack, measured)


def project_kernel(stretch_ref, slot_ref, shift_ref, field_ref, proj_ref, w_ref, i_ref):
    a = stretch_ref[0]
    inv = stretch_ref[1]
    lane = lax.broadcasted_iota(jnp.int32, (8, 128), 1).astype(f32)
    groups = shift_ref.shape[0]

    def weights(g, carry):
        u = lane - shift_ref[g]
        v0 = jnp.floor((u - 1.0) * inv) + 1.0
        t0 = u - a * v0
        taps = (1.0 - t0, 1.0 - jnp.abs(t0 - a), 1.0 + t0 - 2.0 * a, 1.0 + t0 - 3.0 * a)
        for j, w in enumerate(taps):
            v = v0 + float(j)
            w_ref[g, j] = jnp.where((v >= 0.0) & (v <= 127.0), jnp.maximum(w, 0.0), 0.0)
        i_ref[g] = v0.astype(jnp.int32)
        return carry

    lax.fori_loop(0, groups, weights, 0)
    proj_ref[...] = jnp.zeros_like(proj_ref)

    def slots(g, carry):
        sums = []
        for j in range(8):
            f = field_ref[slot_ref[1, g * 8 + j]]
            i0 = jnp.broadcast_to(i_ref[g, j : j + 1, :], (8, 128))
            parts = []
            for k in range(4):
                w = jnp.broadcast_to(w_ref[g, k, j : j + 1, :], (8, 128))
                parts.append(jnp.take_along_axis(f, (i0 + k) & 127, axis=1, mode="promise_in_bounds") * w)
            sums.append((parts[0] + parts[1]) + (parts[2] + parts[3]))
        for j in range(8):
            p = slot_ref[0, g * 8 + j]
            proj_ref[p] = proj_ref[p] + sums[j]
        return carry

    lax.fori_loop(0, groups, slots, 0)


def back_kernel(stretch_ref, slot_ref, shift_ref, misfit_ref, back_ref, w_ref, i_ref):
    a = stretch_ref[0]
    lane = lax.broadcasted_iota(jnp.int32, (8, 128), 1).astype(f32)
    groups = shift_ref.shape[0]

    def weights(g, carry):
        t = shift_ref[g] + a * lane
        p0 = jnp.floor(t)
        w1 = t - p0
        w_ref[g, 0] = jnp.where(p0 <= 127.0, 1.0 - w1, 0.0)
        w_ref[g, 1] = jnp.where(p0 <= 126.0, w1, 0.0)
        i_ref[g] = p0.astype(jnp.int32)
        return carry

    lax.fori_loop(0, groups, weights, 0)
    back_ref[...] = jnp.zeros_like(back_ref)

    def slots(g, carry):
        sums = []
        for j in range(8):
            m = misfit_ref[slot_ref[0, g * 8 + j]]
            i0 = jnp.broadcast_to(i_ref[g, j : j + 1, :], (8, 128))
            parts = []
            for k in range(2):
                w = jnp.broadcast_to(w_ref[g, k, j : j + 1, :], (8, 128))
                parts.append(jnp.take_along_axis(m, (i0 + k) & 127, axis=1, mode="promise_in_bounds") * w)
            sums.append(parts[0] + parts[1])
        for j in range(8):
            q = slot_ref[1, g * 8 + j]
            back_ref[q] = back_ref[q] + sums[j]
        return carry

    lax.fori_loop(0, groups, slots, 0)


def rays(body, taps, name, stretch2, slots, shifts, rows):
    groups = shifts.shape[0]
    return pl.pallas_call(
        body,
        out_shape=jax.ShapeDtypeStruct((128, 8, 128), f32),
        in_specs=[SM, SM, VM, VM],
        out_specs=VM,
        scratch_shapes=[pltpu.VMEM((groups, taps, 8, 128), f32), pltpu.VMEM((groups, 8, 128), jnp.int32)],
        compiler_params=pltpu.CompilerParams(vmem_limit_bytes=LIMIT),
        name=name,
    )(stretch2, slots, shifts, rows)


def reduce_kernel(
    proj_ref, meas_ref, c_ref,
    mis_ref, own_ref, zlow_ref, zhigh_ref, ylow_ref, yhigh_ref,
    a1, b1, a2, b2, sum_a, sum_b, send_sem, recv_sem,
):
    angle, x, z, half = position()
    slab = (x * 8 + z) * 2 + half
    nb = 4 - NA
    part_a, part_b = pl.ds(0, NA), pl.ds(NA, nb)
    xs = [lax.rem(x + k, 4) for k in range(1, 4)]
    zs = [lax.rem(z + k, 8) for k in range(1, 8)]
    to_x = [device(angle, xx, z, half) for xx in xs]
    to_z = [device(angle, x, zz, half) for zz in zs]
    above = (angle, lax.rem(slab + 1, 64))
    below = (angle, lax.rem(slab + 63, 64))
    right = (lax.rem(angle + 1, 4), slab)
    left = (lax.rem(angle + 3, 4), slab)
    greet(to_x + to_z + [above, below, right, left])

    count = [0]

    def put(src, dst, target):
        k = count[0]
        count[0] += 1
        return send(src, dst, send_sem.at[k], recv_sem.at[k], target)

    first_b = [put(proj_ref.at[:, zs[k], part_b], b1.at[k], to_z[k]) for k in range(7)]
    first_a = [put(proj_ref.at[xs[k], :, part_a], a1.at[k], to_x[k]) for k in range(3)]
    halos = [
        put(c_ref.at[:, pl.ds(1024, 1024)], zlow_ref, above),
        put(c_ref.at[:, pl.ds(0, 1024)], zhigh_ref, below),
    ]
    for s in range(2):
        halos.append(put(c_ref.at[:, pl.ds(s * 1024 + 896, 128)], ylow_ref.at[:, pl.ds(s * 128, 128)], right))
        halos.append(put(c_ref.at[:, pl.ds(s * 1024, 128)], yhigh_ref.at[:, pl.ds(s * 128, 128)], left))

    for copy in first_a:
        copy.wait_recv()
    sum_a[...] = proj_ref[x, :, :NA] + a1[0] + a1[1] + a1[2]
    second_a = [put(sum_a.at[zs[k]], a2.at[k], to_z[k]) for k in range(7)]
    for copy in first_b:
        copy.wait_recv()
    sum_b[...] = proj_ref[:, z, NA:] + ((b1[0] + b1[1]) + (b1[2] + b1[3])) + ((b1[4] + b1[5]) + b1[6])
    second_b = [put(sum_b.at[xs[k]], b2.at[k], to_x[k]) for k in range(3)]
    for copy in second_a:
        copy.wait_recv()
    total_a = sum_a[z] + ((a2[0] + a2[1]) + (a2[2] + a2[3])) + ((a2[4] + a2[5]) + a2[6]) - meas_ref[:NA]
    own_ref[:NA] = total_a
    mis_ref[x, z, :NA] = total_a
    third_a = [put(own_ref.at[part_a], mis_ref.at[x, z, part_a], to_z[k]) for k in range(7)]
    for copy in second_b:
        copy.wait_recv()
    total_b = sum_b[x] + (b2[0] + b2[1]) + b2[2] - meas_ref[NA:]
    own_ref[NA:] = total_b
    mis_ref[x, z, NA:] = total_b
    third_b = [put(own_ref.at[part_b], mis_ref.at[x, z, part_b], to_x[k]) for k in range(3)]
    for copy in third_b:
        copy.wait_recv()
    fourth_b = [put(mis_ref.at[:, z, part_b], mis_ref.at[:, z, part_b], to_z[k]) for k in range(7)]
    for copy in third_a:
        copy.wait_recv()
    fourth_a = [put(mis_ref.at[x, :, part_a], mis_ref.at[x, :, part_a], to_x[k]) for k in range(3)]
    for copy in fourth_a + fourth_b:
        copy.wait_recv()
    for copy in halos:
        copy.wait_recv()
    for copy in first_a + first_b + second_a + second_b + third_a + third_b + fourth_a + fourth_b + halos:
        copy.wait_send()


def reduce(proj, measured, c_own):
    nb = 4 - NA
    return pl.pallas_call(
        reduce_kernel,
        out_shape=(
            jax.ShapeDtypeStruct((4, 8, 4, 8, 128), f32),
            jax.ShapeDtypeStruct((4, 8, 128), f32),
            jax.ShapeDtypeStruct((48, 1024), f32),
            jax.ShapeDtypeStruct((48, 1024), f32),
            jax.ShapeDtypeStruct((48, 256), f32),
            jax.ShapeDtypeStruct((48, 256), f32),
        ),
        in_specs=[VM] * 3,
        out_specs=(VM,) * 6,
        scratch_shapes=[
            pltpu.VMEM((3, 8, NA, 8, 128), f32),
            pltpu.VMEM((7, 4, nb, 8, 128), f32),
            pltpu.VMEM((7, NA, 8, 128), f32),
            pltpu.VMEM((3, nb, 8, 128), f32),
            pltpu.VMEM((8, NA, 8, 128), f32),
            pltpu.VMEM((4, nb, 8, 128), f32),
            pltpu.SemaphoreType.DMA((46,)),
            pltpu.SemaphoreType.DMA((46,)),
        ],
        compiler_params=pltpu.CompilerParams(collective_id=1, has_side_effects=True, vmem_limit_bytes=LIMIT),
        name="reduce",
    )(proj, measured, c_own)


def column_partners(angle, x, z, half):
    found = []
    for k in range(1, 8):
        ta, th = lax.rem(angle + k // 2, 4), lax.rem(half + k % 2, 2)
        found.append((k, ta, th, device(ta, x, z, th)))
    return found


def send_back(back_ref, got, rotation, partners, send_sem, recv_sem):
    copies = []
    for k, ta, th, target in partners:
        src = back_ref.at[pl.ds(pl.multiple_of((k % 2) * 64 + ta * 16, 16), 16)]
        copies.append(send(src, got.at[rotation], send_sem.at[k - 1], recv_sem.at[k - 1], target))
    return copies


def smooth(angle, slab, c_ref, zlow_ref, zhigh_ref, ylow_ref, yhigh_ref, next_ref):
    lane = lax.broadcasted_iota(jnp.int32, (48, 128), 1)
    has_zlow = (slab > 0).astype(f32)
    has_zhigh = (slab < 63).astype(f32)
    has_ylow = (angle > 0).astype(f32)
    has_yhigh = (angle < 3).astype(f32)

    def at(ref, row):
        return ref[:, row * 128 : row * 128 + 128]

    for s in range(2):
        for y in range(8):
            row = s * 8 + y
            c = at(c_ref, row)
            near = at(zlow_ref, y) * has_zlow + at(c_ref, y + 8) if s == 0 else at(c_ref, y) + at(zhigh_ref, y) * has_zhigh
            near += at(c_ref, row - 1) if y > 0 else at(ylow_ref, s) * has_ylow
            near += at(c_ref, row + 1) if y < 7 else at(yhigh_ref, s) * has_yhigh
            near += jnp.where(lane == 0, 0.0, pltpu.roll(c, 1, 1)) + jnp.where(lane == 127, 0.0, pltpu.roll(c, 127, 1))
            next_ref[:, row * 128 : row * 128 + 128] = c - (STEP * SMOOTH) * (6.0 * c - near)


def gradient_step(harm_t, got, next_ref, chunk):
    both = jnp.concatenate([got[:, chunk * 4 + r].reshape(64, 128) for r in range(4)], axis=1)
    cols = pl.ds(chunk * 512, 512)
    new = next_ref[:, cols] - STEP * dot(harm_t, both)
    next_ref[:, cols] = new
    return new


def middle_kernel(
    back_ref, c_ref, harm_ref, harm_t_ref, zlow_ref, zhigh_ref, ylow_ref, yhigh_ref,
    next_ref, field_ref, got, out, send_sem, recv_sem,
):
    angle, x, z, half = position()
    slab = (x * 8 + z) * 2 + half
    rotation = angle * 2 + half
    partners = column_partners(angle, x, z, half)
    greet([target for _, _, _, target in partners])
    copies = send_back(back_ref, got, rotation, partners, send_sem, recv_sem)
    got[rotation] = back_ref[pl.ds(pl.multiple_of(angle * 16, 16), 16)]
    smooth(angle, slab, c_ref, zlow_ref, zhigh_ref, ylow_ref, yhigh_ref, next_ref)
    for copy in copies:
        copy.wait_recv()
    for chunk in range(4):
        new = gradient_step(harm_t_ref[...], got, next_ref, chunk)
        fields = dot(harm_ref[...], new)
        for r in range(4):
            out[:, chunk * 4 + r] = fields[:, r * 128 : r * 128 + 128].reshape(8, 8, 128)
    later = []
    for k, ta, th, target in partners:
        dst = field_ref.at[pl.ds(pl.multiple_of((k % 2) * 64 + angle * 16, 16), 16)]
        later.append(send(out.at[ta * 2 + th], dst, send_sem.at[6 + k], recv_sem.at[6 + k], target))
    field_ref[pl.ds(pl.multiple_of(angle * 16, 16), 16)] = out[rotation]
    for copy in later:
        copy.wait_recv()
    for copy in copies + later:
        copy.wait_send()


def middle(back, c_own, harm_all, harm_t, halos):
    return pl.pallas_call(
        middle_kernel,
        out_shape=(jax.ShapeDtypeStruct((48, 2048), f32), jax.ShapeDtypeStruct((128, 8, 128), f32)),
        in_specs=[VM] * 8,
        out_specs=(VM, VM),
        scratch_shapes=[
            pltpu.VMEM((8, 16, 8, 128), f32),
            pltpu.VMEM((8, 16, 8, 128), f32),
            pltpu.SemaphoreType.DMA((14,)),
            pltpu.SemaphoreType.DMA((14,)),
        ],
        compiler_params=pltpu.CompilerParams(collective_id=2, has_side_effects=True, vmem_limit_bytes=LIMIT),
        name="middle",
    )(back, c_own, harm_all, harm_t, *halos)


def end_kernel(
    back_ref, c_ref, harm_t_ref, zlow_ref, zhigh_ref, ylow_ref, yhigh_ref, own_ref,
    all_ref, mis_ref, next_ref, got, send_sem, recv_sem,
):
    angle, x, z, half = position()
    slab = (x * 8 + z) * 2 + half
    rotation = angle * 2 + half
    other = 1 - half
    partners = column_partners(angle, x, z, half)
    greet([target for _, _, _, target in partners])
    copies = send_back(back_ref, got, rotation, partners, send_sem, recv_sem)
    last = send(own_ref.at[pl.ds(other * 2, 2)], mis_ref.at[half], send_sem.at[7], recv_sem.at[7], device(angle, x, z, other))
    got[rotation] = back_ref[pl.ds(pl.multiple_of(angle * 16, 16), 16)]
    mis_ref[half] = own_ref[pl.ds(half * 2, 2)]
    smooth(angle, slab, c_ref, zlow_ref, zhigh_ref, ylow_ref, yhigh_ref, next_ref)
    for copy in copies:
        copy.wait_recv()
    for chunk in range(4):
        gradient_step(harm_t_ref[...], got, next_ref, chunk)
    later = []
    for k in range(1, 4):
        target = device(lax.rem(angle + k, 4), x, z, half)
        later.append(send(next_ref, all_ref.at[angle], send_sem.at[7 + k], recv_sem.at[7 + k], target))
    all_ref[angle] = next_ref[...]
    for copy in later + [last]:
        copy.wait_recv()
    for copy in copies + later + [last]:
        copy.wait_send()


def end(back, c_own, harm_t, halos, own):
    return pl.pallas_call(
        end_kernel,
        out_shape=(jax.ShapeDtypeStruct((4, 48, 2048), f32), jax.ShapeDtypeStruct((2, 2, 8, 128), f32)),
        in_specs=[VM] * 8,
        out_specs=(VM, VM),
        scratch_shapes=[
            pltpu.VMEM((48, 2048), f32),
            pltpu.VMEM((8, 16, 8, 128), f32),
            pltpu.SemaphoreType.DMA((11,)),
            pltpu.SemaphoreType.DMA((11,)),
        ],
        compiler_params=pltpu.CompilerParams(collective_id=3, has_side_effects=True, vmem_limit_bytes=LIMIT),
        name="end",
    )(back, c_own, harm_t, *halos, own)


def per_device(coefficients, harmonics, stretch, measured, tile_pixel, tile_voxel, tile_shift, tile_count):
    angle = lax.axis_index("angle")
    half = lax.rem(lax.axis_index("slab"), 2)
    tiles = tile_pixel.shape[1]
    c_all = coefficients.reshape(45, 2, 4, 8, 128).transpose(2, 0, 1, 3, 4).reshape(4, 45, 2048)
    c_all = jnp.pad(c_all, ((0, 0), (0, 3), (0, 0)))
    harm = jnp.pad(harmonics.reshape(16, 45), ((0, 0), (0, 83)))
    valid = jnp.arange(tiles)[None, :] < tile_count
    row = lax.rem(lax.div(tile_voxel, 8), 4) * 16 + lax.div(tile_voxel, 32) * 8 + lax.rem(tile_voxel, 8)
    pack = jnp.concatenate(
        [tile_pixel.astype(f32), row.astype(f32), jnp.where(valid, tile_shift, FAR), jnp.zeros((2, tiles), f32)], axis=0
    )
    pack = jnp.pad(pack, ((0, 0), (0, 256 - tiles)))
    field, harm_got, pack_got, meas_got = begin(c_all, harm, pack, measured.reshape(16, 256))

    mine = lax.dynamic_index_in_dim(pack.reshape(4, 2, 256), half, 1, keepdims=False)[:, :tiles]
    theirs = lax.dynamic_index_in_dim(pack_got.reshape(4, 2, 256), half, 1, keepdims=False)[:, :tiles]
    theirs = theirs + jnp.array([[0.0], [64.0], [0.0], [0.0]], f32)
    slots_f = jnp.concatenate([mine, theirs], axis=1)
    slots = slots_f[:2].astype(jnp.int32)
    shifts = jnp.broadcast_to(slots_f[2][:, None], (2 * tiles, 128)).reshape(2 * tiles // 8, 8, 128)
    a = lax.dynamic_index_in_dim(stretch, half, 0, keepdims=False)
    stretch2 = jnp.stack([a, 1.0 / a])
    meas_mine = lax.dynamic_index_in_dim(measured, half, 0, keepdims=False)
    meas_theirs = lax.dynamic_index_in_dim(meas_got.reshape(2, 8, 256), half, 0, keepdims=False)
    pair = jnp.where(half == 0, jnp.stack([meas_mine, meas_theirs]), jnp.stack([meas_theirs, meas_mine]))
    meas = pair.reshape(2, 8, 2, 128).transpose(0, 2, 1, 3).reshape(4, 8, 128)
    harm_all = harm_got.reshape(64, 128)[:, :48]
    harm_t = harm_all.T
    c_own = lax.dynamic_index_in_dim(c_all, angle, 0, keepdims=False)

    for iteration in range(2):
        proj = rays(project_kernel, 4, "project", stretch2, slots, shifts, field)
        mis, own, *halos = reduce(proj.reshape(4, 8, 4, 8, 128), meas, c_own)
        back = rays(back_kernel, 2, "back", stretch2, slots, shifts, mis.reshape(128, 8, 128))
        if iteration == 0:
            c_own, field = middle(back, c_own, harm_all, harm_t, halos)
        else:
            c_new, mis_new = end(back, c_own, harm_t, halos, own)
    updated = c_new[:, :45].reshape(4, 45, 2, 8, 128).transpose(1, 2, 0, 3, 4).reshape(45, 2, 32, 128)
    misfit = mis_new.transpose(0, 2, 1, 3).reshape(2, 8, 256)
    return updated, misfit


def solution(mesh):
    in_specs = (
        P(None, "slab", None, None),
        P("angle", None, None),
        P("angle"),
        P("angle", None, "slab"),
        P("angle", "slab"),
        P("angle", "slab"),
        P("angle", "slab"),
        P("angle", "slab"),
    )
    out_specs = (P(None, "slab", None, None), P("angle", None, "slab"))
    return jax.shard_map(per_device, mesh=mesh, in_specs=in_specs, out_specs=out_specs, check_vma=False)
```

```python
import jax
import jax.numpy as jnp
from jax import lax
from jax.experimental import pallas as pl
from jax.experimental.pallas import tpu as pltpu
from jax.sharding import PartitionSpec as P

f32 = jnp.float32
MESH = pl.DeviceIdType.MESH
STEP = 0.003
SMOOTH = 6.0
NA = 2
FAR = 1.0e6

VM = pl.BlockSpec(memory_space=pltpu.VMEM)
SM = pl.BlockSpec(memory_space=pltpu.SMEM)
LIMIT = 48 * 2**20
DN = lax.GatherDimensionNumbers(
    offset_dims=(), collapsed_slice_dims=(1,), start_index_map=(1,), operand_batching_dims=(0,), start_indices_batching_dims=(0,)
)


def position():
    angle = lax.axis_index("angle")
    slab = lax.axis_index("slab")
    return angle, lax.div(slab, 16), lax.rem(lax.div(slab, 2), 8), lax.rem(slab, 2)


def device(angle, x, z, half):
    return (angle, (x * 8 + z) * 2 + half)


def greet(partners):
    barrier = pltpu.get_barrier_semaphore()
    for partner in partners:
        pl.semaphore_signal(barrier, inc=1, device_id=partner, device_id_type=MESH)
    pl.semaphore_wait(barrier, len(partners))


def send(src, dst, send_sem, recv_sem, target):
    copy = pltpu.make_async_remote_copy(
        src_ref=src, dst_ref=dst, send_sem=send_sem, recv_sem=recv_sem, device_id=target, device_id_type=MESH
    )
    copy.start()
    return copy


def dot(a, b):
    return jnp.dot(a, b, preferred_element_type=f32, precision=lax.Precision.HIGHEST)


def begin_kernel(c_ref, harm_ref, pack_ref, meas_ref, field_ref, harm_all_ref, pack_got, meas_got, out_ref, send_sem, recv_sem):
    angle, x, z, half = position()
    other = 1 - half
    partner = device(angle, x, z, other)
    peers = [device(lax.rem(angle + k, 4), x, z, half) for k in range(1, 4)]
    greet([partner] + peers)
    copies = [
        send(pack_ref, pack_got, send_sem.at[0], recv_sem.at[0], partner),
        send(meas_ref, meas_got, send_sem.at[1], recv_sem.at[1], partner),
    ]
    for k, peer in enumerate(peers):
        copies.append(send(harm_ref, harm_all_ref.at[angle], send_sem.at[2 + k], recv_sem.at[2 + k], peer))
    harm_all_ref[angle] = harm_ref[...]

    def fields(which, dest, base):
        rows = harm_ref[pl.ds(pl.multiple_of(which * 8, 8), 8), :][:, :48]
        for chunk in range(4):
            out = dot(rows, c_ref[chunk])
            for row in range(16):
                dest[base + chunk * 16 + row] = out[:, row * 128 : row * 128 + 128]

    fields(other, out_ref, 0)
    copies.append(send(out_ref, field_ref.at[pl.ds(64, 64)], send_sem.at[5], recv_sem.at[5], partner))
    fields(half, field_ref, 0)
    for copy in copies:
        copy.wait()


def begin(c_all, harm, pack, measured):
    return pl.pallas_call(
        begin_kernel,
        out_shape=(
            jax.ShapeDtypeStruct((128, 8, 128), f32),
            jax.ShapeDtypeStruct((4, 16, 128), f32),
            jax.ShapeDtypeStruct(pack.shape, f32),
            jax.ShapeDtypeStruct(measured.shape, f32),
        ),
        in_specs=[VM] * 4,
        out_specs=(VM,) * 4,
        scratch_shapes=[pltpu.VMEM((64, 8, 128), f32), pltpu.SemaphoreType.DMA((6,)), pltpu.SemaphoreType.DMA((6,))],
        compiler_params=pltpu.CompilerParams(collective_id=0, has_side_effects=True, vmem_limit_bytes=LIMIT),
        name="begin",
    )(c_all, harm, pack, measured)


def project_kernel(stretch_ref, slot_ref, shift_ref, field_ref, proj_ref, w_ref, i_ref):
    a = stretch_ref[0]
    inv = stretch_ref[1]
    lane = lax.broadcasted_iota(jnp.int32, (8, 128), 1).astype(f32)
    groups = shift_ref.shape[0]

    def weights(g, carry):
        u = lane - shift_ref[g]
        v0 = jnp.floor((u - 1.0) * inv) + 1.0
        t0 = u - a * v0
        taps = (1.0 - t0, 1.0 - jnp.abs(t0 - a), 1.0 + t0 - 2.0 * a, 1.0 + t0 - 3.0 * a)
        for j, w in enumerate(taps):
            v = v0 + float(j)
            w_ref[g, j] = jnp.where((v >= 0.0) & (v <= 127.0), jnp.maximum(w, 0.0), 0.0)
        i_ref[g] = v0.astype(jnp.int32)
        return carry

    lax.fori_loop(0, groups, weights, 0)
    proj_ref[...] = jnp.zeros_like(proj_ref)

    def slots(g, carry):
        sums = []
        for j in range(8):
            f = field_ref[slot_ref[1, g * 8 + j]]
            i0 = jnp.broadcast_to(i_ref[g, j : j + 1, :], (8, 128))
            parts = []
            for k in range(4):
                w = jnp.broadcast_to(w_ref[g, k, j : j + 1, :], (8, 128))
                parts.append(jnp.take_along_axis(f, (i0 + k) & 127, axis=1, mode="promise_in_bounds") * w)
            sums.append((parts[0] + parts[1]) + (parts[2] + parts[3]))
        for j in range(8):
            p = slot_ref[0, g * 8 + j]
            proj_ref[p] = proj_ref[p] + sums[j]
        return carry

    lax.fori_loop(0, groups, slots, 0)


def back_kernel(stretch_ref, slot_ref, shift_ref, misfit_ref, back_ref, w_ref, i_ref):
    a = stretch_ref[0]
    lane = lax.broadcasted_iota(jnp.int32, (8, 128), 1).astype(f32)
    groups = shift_ref.shape[0]

    def weights(g, carry):
        t = shift_ref[g] + a * lane
        p0 = jnp.floor(t)
        w1 = t - p0
        w_ref[g, 0] = jnp.where(p0 <= 127.0, 1.0 - w1, 0.0)
        w_ref[g, 1] = jnp.where(p0 <= 126.0, w1, 0.0)
        i_ref[g] = p0.astype(jnp.int32)
        return carry

    lax.fori_loop(0, groups, weights, 0)
    back_ref[...] = jnp.zeros_like(back_ref)

    def slots(g, carry):
        sums = []
        for j in range(8):
            m = misfit_ref[slot_ref[0, g * 8 + j]]
            i0 = jnp.broadcast_to(i_ref[g, j : j + 1, :], (8, 128))
            parts = []
            for k in range(2):
                w = jnp.broadcast_to(w_ref[g, k, j : j + 1, :], (8, 128))
                parts.append(jnp.take_along_axis(m, (i0 + k) & 127, axis=1, mode="promise_in_bounds") * w)
            sums.append(parts[0] + parts[1])
        for j in range(8):
            q = slot_ref[1, g * 8 + j]
            back_ref[q] = back_ref[q] + sums[j]
        return carry

    lax.fori_loop(0, groups, slots, 0)


def rays(body, taps, name, stretch2, slots, shifts, rows):
    groups = shifts.shape[0]
    return pl.pallas_call(
        body,
        out_shape=jax.ShapeDtypeStruct((128, 8, 128), f32),
        in_specs=[SM, SM, VM, VM],
        out_specs=VM,
        scratch_shapes=[pltpu.VMEM((groups, taps, 8, 128), f32), pltpu.VMEM((groups, 8, 128), jnp.int32)],
        compiler_params=pltpu.CompilerParams(vmem_limit_bytes=LIMIT),
        name=name,
    )(stretch2, slots, shifts, rows)


def reduce_kernel(
    proj_ref, meas_ref, c_ref,
    mis_ref, own_ref, zlow_ref, zhigh_ref, ylow_ref, yhigh_ref,
    a1, b1, a2, b2, sum_a, sum_b, send_sem, recv_sem,
):
    angle, x, z, half = position()
    slab = (x * 8 + z) * 2 + half
    nb = 4 - NA
    part_a, part_b = pl.ds(0, NA), pl.ds(NA, nb)
    xs = [lax.rem(x + k, 4) for k in range(1, 4)]
    zs = [lax.rem(z + k, 8) for k in range(1, 8)]
    to_x = [device(angle, xx, z, half) for xx in xs]
    to_z = [device(angle, x, zz, half) for zz in zs]
    above = (angle, lax.rem(slab + 1, 64))
    below = (angle, lax.rem(slab + 63, 64))
    right = (lax.rem(angle + 1, 4), slab)
    left = (lax.rem(angle + 3, 4), slab)
    greet(to_x + to_z + [above, below, right, left])

    count = [0]

    def put(src, dst, target):
        k = count[0]
        count[0] += 1
        return send(src, dst, send_sem.at[k], recv_sem.at[k], target)

    first_b = [put(proj_ref.at[:, zs[k], part_b], b1.at[k], to_z[k]) for k in range(7)]
    first_a = [put(proj_ref.at[xs[k], :, part_a], a1.at[k], to_x[k]) for k in range(3)]
    halos = [
        put(c_ref.at[:, pl.ds(1024, 1024)], zlow_ref, above),
        put(c_ref.at[:, pl.ds(0, 1024)], zhigh_ref, below),
    ]
    for s in range(2):
        halos.append(put(c_ref.at[:, pl.ds(s * 1024 + 896, 128)], ylow_ref.at[:, pl.ds(s * 128, 128)], right))
        halos.append(put(c_ref.at[:, pl.ds(s * 1024, 128)], yhigh_ref.at[:, pl.ds(s * 128, 128)], left))

    for copy in first_a:
        copy.wait_recv()
    sum_a[...] = proj_ref[x, :, :NA] + a1[0] + a1[1] + a1[2]
    second_a = [put(sum_a.at[zs[k]], a2.at[k], to_z[k]) for k in range(7)]
    for copy in first_b:
        copy.wait_recv()
    sum_b[...] = proj_ref[:, z, NA:] + ((b1[0] + b1[1]) + (b1[2] + b1[3])) + ((b1[4] + b1[5]) + b1[6])
    second_b = [put(sum_b.at[xs[k]], b2.at[k], to_x[k]) for k in range(3)]
    for copy in second_a:
        copy.wait_recv()
    total_a = sum_a[z] + ((a2[0] + a2[1]) + (a2[2] + a2[3])) + ((a2[4] + a2[5]) + a2[6]) - meas_ref[:NA]
    own_ref[:NA] = total_a
    mis_ref[x, z, :NA] = total_a
    third_a = [put(own_ref.at[part_a], mis_ref.at[x, z, part_a], to_z[k]) for k in range(7)]
    for copy in second_b:
        copy.wait_recv()
    total_b = sum_b[x] + (b2[0] + b2[1]) + b2[2] - meas_ref[NA:]
    own_ref[NA:] = total_b
    mis_ref[x, z, NA:] = total_b
    third_b = [put(own_ref.at[part_b], mis_ref.at[x, z, part_b], to_x[k]) for k in range(3)]
    for copy in third_b:
        copy.wait_recv()
    fourth_b = [put(mis_ref.at[:, z, part_b], mis_ref.at[:, z, part_b], to_z[k]) for k in range(7)]
    for copy in third_a:
        copy.wait_recv()
    fourth_a = [put(mis_ref.at[x, :, part_a], mis_ref.at[x, :, part_a], to_x[k]) for k in range(3)]
    for copy in fourth_a + fourth_b:
        copy.wait_recv()
    for copy in halos:
        copy.wait_recv()
    for copy in first_a + first_b + second_a + second_b + third_a + third_b + fourth_a + fourth_b + halos:
        copy.wait_send()


def reduce(proj, measured, c_own):
    nb = 4 - NA
    return pl.pallas_call(
        reduce_kernel,
        out_shape=(
            jax.ShapeDtypeStruct((4, 8, 4, 8, 128), f32),
            jax.ShapeDtypeStruct((4, 8, 128), f32),
            jax.ShapeDtypeStruct((48, 1024), f32),
            jax.ShapeDtypeStruct((48, 1024), f32),
            jax.ShapeDtypeStruct((48, 256), f32),
            jax.ShapeDtypeStruct((48, 256), f32),
        ),
        in_specs=[VM] * 3,
        out_specs=(VM,) * 6,
        scratch_shapes=[
            pltpu.VMEM((3, 8, NA, 8, 128), f32),
            pltpu.VMEM((7, 4, nb, 8, 128), f32),
            pltpu.VMEM((7, NA, 8, 128), f32),
            pltpu.VMEM((3, nb, 8, 128), f32),
            pltpu.VMEM((8, NA, 8, 128), f32),
            pltpu.VMEM((4, nb, 8, 128), f32),
            pltpu.SemaphoreType.DMA((46,)),
            pltpu.SemaphoreType.DMA((46,)),
        ],
        compiler_params=pltpu.CompilerParams(collective_id=1, has_side_effects=True, vmem_limit_bytes=LIMIT),
        name="reduce",
    )(proj, measured, c_own)


def column_partners(angle, x, z, half):
    found = []
    for k in range(1, 8):
        ta, th = lax.rem(angle + k // 2, 4), lax.rem(half + k % 2, 2)
        found.append((k, ta, th, device(ta, x, z, th)))
    return found


def send_back(back_ref, got, rotation, partners, send_sem, recv_sem):
    copies = []
    for k, ta, th, target in partners:
        src = back_ref.at[pl.ds(pl.multiple_of((k % 2) * 64 + ta * 16, 16), 16)]
        copies.append(send(src, got.at[rotation], send_sem.at[k - 1], recv_sem.at[k - 1], target))
    return copies


def smooth(angle, slab, c_ref, zlow_ref, zhigh_ref, ylow_ref, yhigh_ref, next_ref):
    lane = lax.broadcasted_iota(jnp.int32, (48, 128), 1)
    has_zlow = (slab > 0).astype(f32)
    has_zhigh = (slab < 63).astype(f32)
    has_ylow = (angle > 0).astype(f32)
    has_yhigh = (angle < 3).astype(f32)

    def at(ref, row):
        return ref[:, row * 128 : row * 128 + 128]

    for s in range(2):
        for y in range(8):
            row = s * 8 + y
            c = at(c_ref, row)
            near = at(zlow_ref, y) * has_zlow + at(c_ref, y + 8) if s == 0 else at(c_ref, y) + at(zhigh_ref, y) * has_zhigh
            near += at(c_ref, row - 1) if y > 0 else at(ylow_ref, s) * has_ylow
            near += at(c_ref, row + 1) if y < 7 else at(yhigh_ref, s) * has_yhigh
            near += jnp.where(lane == 0, 0.0, pltpu.roll(c, 1, 1)) + jnp.where(lane == 127, 0.0, pltpu.roll(c, 127, 1))
            next_ref[:, row * 128 : row * 128 + 128] = c - (STEP * SMOOTH) * (6.0 * c - near)


def gradient_step(harm_t, got, next_ref, chunk):
    both = jnp.concatenate([got[:, chunk * 4 + r].reshape(64, 128) for r in range(4)], axis=1)
    cols = pl.ds(chunk * 512, 512)
    new = next_ref[:, cols] - STEP * dot(harm_t, both)
    next_ref[:, cols] = new
    return new


def middle_kernel(
    back_ref, c_ref, harm_ref, harm_t_ref, zlow_ref, zhigh_ref, ylow_ref, yhigh_ref,
    next_ref, field_ref, got, out, send_sem, recv_sem,
):
    angle, x, z, half = position()
    slab = (x * 8 + z) * 2 + half
    rotation = angle * 2 + half
    partners = column_partners(angle, x, z, half)
    greet([target for _, _, _, target in partners])
    copies = send_back(back_ref, got, rotation, partners, send_sem, recv_sem)
    got[rotation] = back_ref[pl.ds(pl.multiple_of(angle * 16, 16), 16)]
    smooth(angle, slab, c_ref, zlow_ref, zhigh_ref, ylow_ref, yhigh_ref, next_ref)
    for copy in copies:
        copy.wait_recv()
    probe = c_ref[0:8, 0:128]
    i0 = jnp.floor(probe).astype(jnp.int32) & 127
    picked = lax.gather(probe, i0[..., None], DN, slice_sizes=(1, 1), mode=lax.GatherScatterMode.PROMISE_IN_BOUNDS)
    ids = lax.broadcasted_iota(jnp.int32, (64, 64), 1)
    hot = jnp.where(ids == i0[0:1, :64], 1.0, 0.0).astype(jnp.bfloat16)
    hit = jnp.dot(hot, got[0, 0:8, :, :].reshape(64, 128).astype(jnp.bfloat16), preferred_element_type=f32)

    def step(i, carry):
        next_ref[pl.ds(pl.multiple_of(i * 8, 8), 8), :128] += jnp.minimum(jnp.abs(picked + hit[:8]), 0.0)
        return carry

    lax.fori_loop(0, 6, step, 0)
    for chunk in range(4):
        new = gradient_step(harm_t_ref[...], got, next_ref, chunk)
        fields = dot(harm_ref[...], new)
        for r in range(4):
            out[:, chunk * 4 + r] = fields[:, r * 128 : r * 128 + 128].reshape(8, 8, 128)
    later = []
    for k, ta, th, target in partners:
        dst = field_ref.at[pl.ds(pl.multiple_of((k % 2) * 64 + angle * 16, 16), 16)]
        later.append(send(out.at[ta * 2 + th], dst, send_sem.at[6 + k], recv_sem.at[6 + k], target))
    field_ref[pl.ds(pl.multiple_of(angle * 16, 16), 16)] = out[rotation]
    for copy in later:
        copy.wait_recv()
    for copy in copies + later:
        copy.wait_send()


def middle(back, c_own, harm_all, harm_t, halos):
    return pl.pallas_call(
        middle_kernel,
        out_shape=(jax.ShapeDtypeStruct((48, 2048), f32), jax.ShapeDtypeStruct((128, 8, 128), f32)),
        in_specs=[VM] * 8,
        out_specs=(VM, VM),
        scratch_shapes=[
            pltpu.VMEM((8, 16, 8, 128), f32),
            pltpu.VMEM((8, 16, 8, 128), f32),
            pltpu.SemaphoreType.DMA((14,)),
            pltpu.SemaphoreType.DMA((14,)),
        ],
        compiler_params=pltpu.CompilerParams(collective_id=2, has_side_effects=True, vmem_limit_bytes=LIMIT),
        name="middle",
    )(back, c_own, harm_all, harm_t, *halos)


def end_kernel(
    back_ref, c_ref, harm_t_ref, zlow_ref, zhigh_ref, ylow_ref, yhigh_ref, own_ref,
    all_ref, mis_ref, next_ref, got, send_sem, recv_sem,
):
    angle, x, z, half = position()
    slab = (x * 8 + z) * 2 + half
    rotation = angle * 2 + half
    other = 1 - half
    partners = column_partners(angle, x, z, half)
    greet([target for _, _, _, target in partners])
    copies = send_back(back_ref, got, rotation, partners, send_sem, recv_sem)
    last = send(own_ref.at[pl.ds(other * 2, 2)], mis_ref.at[half], send_sem.at[7], recv_sem.at[7], device(angle, x, z, other))
    got[rotation] = back_ref[pl.ds(pl.multiple_of(angle * 16, 16), 16)]
    mis_ref[half] = own_ref[pl.ds(half * 2, 2)]
    smooth(angle, slab, c_ref, zlow_ref, zhigh_ref, ylow_ref, yhigh_ref, next_ref)
    for copy in copies:
        copy.wait_recv()
    for chunk in range(4):
        gradient_step(harm_t_ref[...], got, next_ref, chunk)
    later = []
    for k in range(1, 4):
        target = device(lax.rem(angle + k, 4), x, z, half)
        later.append(send(next_ref, all_ref.at[angle], send_sem.at[7 + k], recv_sem.at[7 + k], target))
    all_ref[angle] = next_ref[...]
    for copy in later + [last]:
        copy.wait_recv()
    for copy in copies + later + [last]:
        copy.wait_send()


def end(back, c_own, harm_t, halos, own):
    return pl.pallas_call(
        end_kernel,
        out_shape=(jax.ShapeDtypeStruct((4, 48, 2048), f32), jax.ShapeDtypeStruct((2, 2, 8, 128), f32)),
        in_specs=[VM] * 8,
        out_specs=(VM, VM),
        scratch_shapes=[
            pltpu.VMEM((48, 2048), f32),
            pltpu.VMEM((8, 16, 8, 128), f32),
            pltpu.SemaphoreType.DMA((11,)),
            pltpu.SemaphoreType.DMA((11,)),
        ],
        compiler_params=pltpu.CompilerParams(collective_id=3, has_side_effects=True, vmem_limit_bytes=LIMIT),
        name="end",
    )(back, c_own, harm_t, *halos, own)


def per_device(coefficients, harmonics, stretch, measured, tile_pixel, tile_voxel, tile_shift, tile_count):
    angle = lax.axis_index("angle")
    half = lax.rem(lax.axis_index("slab"), 2)
    tiles = tile_pixel.shape[1]
    c_all = coefficients.reshape(45, 2, 4, 8, 128).transpose(2, 0, 1, 3, 4).reshape(4, 45, 2048)
    c_all = jnp.pad(c_all, ((0, 0), (0, 3), (0, 0)))
    harm = jnp.pad(harmonics.reshape(16, 45), ((0, 0), (0, 83)))
    valid = jnp.arange(tiles)[None, :] < tile_count
    row = lax.rem(lax.div(tile_voxel, 8), 4) * 16 + lax.div(tile_voxel, 32) * 8 + lax.rem(tile_voxel, 8)
    pack = jnp.concatenate(
        [tile_pixel.astype(f32), row.astype(f32), jnp.where(valid, tile_shift, FAR), jnp.zeros((2, tiles), f32)], axis=0
    )
    pack = jnp.pad(pack, ((0, 0), (0, 256 - tiles)))
    field, harm_got, pack_got, meas_got = begin(c_all, harm, pack, measured.reshape(16, 256))

    mine = lax.dynamic_index_in_dim(pack.reshape(4, 2, 256), half, 1, keepdims=False)[:, :tiles]
    theirs = lax.dynamic_index_in_dim(pack_got.reshape(4, 2, 256), half, 1, keepdims=False)[:, :tiles]
    theirs = theirs + jnp.array([[0.0], [64.0], [0.0], [0.0]], f32)
    slots_f = jnp.concatenate([mine, theirs], axis=1)
    slots = slots_f[:2].astype(jnp.int32)
    shifts = jnp.broadcast_to(slots_f[2][:, None], (2 * tiles, 128)).reshape(2 * tiles // 8, 8, 128)
    a = lax.dynamic_index_in_dim(stretch, half, 0, keepdims=False)
    stretch2 = jnp.stack([a, 1.0 / a])
    meas_mine = lax.dynamic_index_in_dim(measured, half, 0, keepdims=False)
    meas_theirs = lax.dynamic_index_in_dim(meas_got.reshape(2, 8, 256), half, 0, keepdims=False)
    pair = jnp.where(half == 0, jnp.stack([meas_mine, meas_theirs]), jnp.stack([meas_theirs, meas_mine]))
    meas = pair.reshape(2, 8, 2, 128).transpose(0, 2, 1, 3).reshape(4, 8, 128)
    harm_all = harm_got.reshape(64, 128)[:, :48]
    harm_t = harm_all.T
    c_own = lax.dynamic_index_in_dim(c_all, angle, 0, keepdims=False)

    for iteration in range(2):
        proj = rays(project_kernel, 4, "project", stretch2, slots, shifts, field)
        mis, own, *halos = reduce(proj.reshape(4, 8, 4, 8, 128), meas, c_own)
        back = rays(back_kernel, 2, "back", stretch2, slots, shifts, mis.reshape(128, 8, 128))
        if iteration == 0:
            c_own, field = middle(back, c_own, harm_all, harm_t, halos)
        else:
            c_new, mis_new = end(back, c_own, harm_t, halos, own)
    updated = c_new[:, :45].reshape(4, 45, 2, 8, 128).transpose(1, 2, 0, 3, 4).reshape(45, 2, 32, 128)
    misfit = mis_new.transpose(0, 2, 1, 3).reshape(2, 8, 256)
    return updated, misfit


def solution(mesh):
    in_specs = (
        P(None, "slab", None, None),
        P("angle", None, None),
        P("angle"),
        P("angle", None, "slab"),
        P("angle", "slab"),
        P("angle", "slab"),
        P("angle", "slab"),
        P("angle", "slab"),
    )
    out_specs = (P(None, "slab", None, None), P("angle", None, "slab"))
    return jax.shard_map(per_device, mesh=mesh, in_specs=in_specs, out_specs=out_specs, check_vma=False)
```

```python
import jax
import jax.numpy as jnp
from jax import lax
from jax.experimental import pallas as pl
from jax.experimental.pallas import tpu as pltpu
from jax.sharding import PartitionSpec as P

f32 = jnp.float32
bf16 = jnp.bfloat16
MESH = pl.DeviceIdType.MESH
STEP = 0.003
SMOOTH = 6.0
FAR = 1.0e6
TS = 192
CHUNK = 48
TAKE = lax.GatherDimensionNumbers(
    offset_dims=(), collapsed_slice_dims=(1,), start_index_map=(1,), operand_batching_dims=(0,), start_indices_batching_dims=(0,)
)

VM = pl.BlockSpec(memory_space=pltpu.VMEM)
SM = pl.BlockSpec(memory_space=pltpu.SMEM)
LIMIT = 48 * 2**20


def position():
    angle = lax.axis_index("angle")
    slab = lax.axis_index("slab")
    return angle, lax.div(slab, 16), lax.rem(lax.div(slab, 2), 8), lax.rem(slab, 2)


def device(angle, x, z, half):
    return (angle, (x * 8 + z) * 2 + half)


def signal(partners):
    barrier = pltpu.get_barrier_semaphore()
    for partner in partners:
        pl.semaphore_signal(barrier, inc=1, device_id=partner, device_id_type=MESH)


def await_signals(partners):
    pl.semaphore_wait(pltpu.get_barrier_semaphore(), len(partners))


def send(src, dst, send_sem, recv_sem, target):
    pltpu.make_async_remote_copy(
        src_ref=src, dst_ref=dst, send_sem=send_sem, recv_sem=recv_sem, device_id=target, device_id_type=MESH
    ).start()


def drain(like, sem):
    pltpu.make_async_copy(like, like, sem).wait()


def dot(a, b):
    return jnp.dot(a, b, preferred_element_type=f32, precision=lax.Precision.HIGHEST)


def hot(a, b):
    return jnp.dot(a, b, preferred_element_type=f32)


def parts(value, count):
    found = []
    for _ in range(count - 1):
        part = value.astype(bf16)
        found.append(part)
        value = value - part.astype(f32)
    return found + [value.astype(bf16)]


def take(values, lanes):
    return lax.gather(values, lanes[..., None], TAKE, slice_sizes=(1, 1), mode=lax.GatherScatterMode.PROMISE_IN_BOUNDS)


def begin_kernel(
    harm_s, c_ref, harm_ref, pix_ref, vox_ref, shift_ref, count_ref, meas_ref,
    field_ref, harm_all_ref, packs_ref, own_ref, blocks, pack, send_sem, recv_sem,
):
    angle, x, z, half = position()
    slab = x * 2 + half
    peers = [device(angle, lax.rem(x + k // 2, 4), z, lax.rem(half + k % 2, 2)) for k in range(1, 8)]
    angles = [device(lax.rem(angle + k, 4), x, z, half) for k in range(1, 4)]
    signal(peers + angles)

    valid = lax.broadcasted_iota(jnp.int32, (2, TS), 1) < count_ref[...]
    pack[...] = jnp.zeros_like(pack)
    pack[0:2, :TS] = pix_ref[...].astype(f32)
    pack[2:4, :TS] = vox_ref[...].astype(f32)
    pack[4:6, :TS] = jnp.where(valid, shift_ref[...], FAR)
    pack[8:16] = meas_ref[0]
    pack[16:24] = meas_ref[1]
    packs_ref[slab] = pack[...]
    harm_all_ref[angle] = jnp.zeros((16, 128), f32)
    harm_all_ref[angle, 0:8, 0:45] = harm_ref[0]
    harm_all_ref[angle, 8:16, 0:45] = harm_ref[1]
    quarter = pl.ds(pl.multiple_of(angle * 8, 8), 8)
    own_ref[:45, :, 0:128] = c_ref[:, 0, quarter, :]
    own_ref[:45, :, 128:256] = c_ref[:, 1, quarter, :]
    own_ref[45:] = jnp.zeros((3, 8, 256), f32)
    await_signals(peers + angles)
    for target in peers:
        send(pack, packs_ref.at[slab], send_sem.at[0], recv_sem.at[0], target)
    for target in angles:
        send(harm_all_ref.at[angle], harm_all_ref.at[angle], send_sem.at[1], recv_sem.at[1], target)

    def fields(which, segments, dest):
        for s in range(2):
            channel = which * 8 + segments * 2 + s
            for zz in range(2):
                sums = [None] * 4
                for k in range(45):
                    h = harm_s[channel, k]
                    for y in range(4):
                        term = c_ref[k, zz, y * 8 : y * 8 + 8, :] * h
                        sums[y] = term if k == 0 else sums[y] + term
                for y in range(4):
                    dest[y, s, :, zz * 128 : zz * 128 + 128] = sums[y]

    def block(i, carry):
        xx, hh = lax.rem(x + lax.div(i, 2), 4), lax.rem(half + lax.rem(i, 2), 2)
        fields(hh, xx, blocks.at[i - 1])
        send(blocks.at[i - 1], field_ref.at[slab], send_sem.at[2], recv_sem.at[2], device(angle, xx, z, hh))
        return carry

    lax.fori_loop(1, 8, block, 0)
    fields(half, x, field_ref.at[slab])
    for sems in (recv_sem, send_sem):
        drain(packs_ref.at[pl.ds(0, 7)], sems.at[0])
        drain(harm_all_ref.at[pl.ds(0, 3)], sems.at[1])
        drain(field_ref.at[pl.ds(0, 7)], sems.at[2])


def begin(coefficients, harmonics, tile_pixel, tile_voxel, tile_shift, tile_count, measured):
    return pl.pallas_call(
        begin_kernel,
        out_shape=(
            jax.ShapeDtypeStruct((8, 4, 2, 8, 256), f32),
            jax.ShapeDtypeStruct((4, 16, 128), f32),
            jax.ShapeDtypeStruct((8, 24, 256), f32),
            jax.ShapeDtypeStruct((48, 8, 256), f32),
        ),
        in_specs=[SM] + [VM] * 7,
        out_specs=(VM,) * 4,
        scratch_shapes=[
            pltpu.VMEM((7, 4, 2, 8, 256), f32),
            pltpu.VMEM((24, 256), f32),
            pltpu.SemaphoreType.DMA((3,)),
            pltpu.SemaphoreType.DMA((3,)),
        ],
        compiler_params=pltpu.CompilerParams(collective_id=0, has_side_effects=True, vmem_limit_bytes=LIMIT),
        name="begin",
    )(harmonics.reshape(16, 45), coefficients, harmonics, tile_pixel, tile_voxel, tile_shift, tile_count, measured)


def project_slab(sl, a, inv, shift_ref, pick_ref, field, picked, contrib):
    rows = [
        jnp.concatenate([field[sl, y, s, :, zz * 128 : zz * 128 + 128] for s in range(2)], axis=1)
        for zz in range(2)
        for y in range(4)
    ]
    split = jnp.concatenate(parts(jnp.concatenate(rows, axis=0), 3), axis=0)
    picked[...] = hot(pick_ref[pl.ds(pl.multiple_of(sl * TS, TS), TS), :], split)
    lane = lax.broadcasted_iota(jnp.int32, (CHUNK, 128), 1).astype(f32)
    for c in range(TS // CHUNK):
        at = pl.ds(pl.multiple_of(sl * TS + c * CHUNK, 16), CHUNK)
        u = lane - shift_ref[at, :]
        v0 = jnp.floor((u - 1.0) * inv) + 1.0
        t0 = u - a * v0
        first = v0.astype(jnp.int32)
        taps = (1.0 - t0, 1.0 - jnp.abs(t0 - a), 1.0 + t0 - 2.0 * a, 1.0 + t0 - 3.0 * a)
        lanes, weights = [], []
        for k in range(4):
            v = first + k
            inside = v & 127
            lanes.append(inside)
            weights.append(jnp.where(v == inside, jnp.maximum(taps[k], 0.0), 0.0))
        for s in range(2):
            f = picked[c * CHUNK : (c + 1) * CHUNK, s * 128 : s * 128 + 128]
            terms = [take(f, lanes[k]) * weights[k] for k in range(4)]
            contrib[at, s * 128 : s * 128 + 128] = (terms[0] + terms[1]) + (terms[2] + terms[3])


def back_slab(sl, a, shift_ref, pick_ref, sum_ref, split, picked, contrib, back):
    picked[...] = hot(pick_ref[pl.ds(pl.multiple_of(sl * TS, TS), TS), :], split[...])
    lane = lax.broadcasted_iota(jnp.int32, (CHUNK, 128), 1).astype(f32)
    for c in range(TS // CHUNK):
        at = slice(c * CHUNK, (c + 1) * CHUNK)
        t = shift_ref[pl.ds(pl.multiple_of(sl * TS + c * CHUNK, 16), CHUNK), :] + a * lane
        p0 = jnp.floor(t)
        w1 = t - p0
        w0 = jnp.where(p0 <= 127.0, 1.0 - w1, 0.0)
        w1 = jnp.where(p0 <= 126.0, w1, 0.0)
        first = p0.astype(jnp.int32)
        lane0, lane1 = first & 127, (first + 1) & 127
        for s in range(2):
            m = picked[at, s * 128 : s * 128 + 128]
            contrib[at, s * 128 : s * 128 + 128] = take(m, lane0) * w0 + take(m, lane1) * w1
    high, low = parts(contrib[:TS], 2)
    total = hot(sum_ref[sl], high) + hot(sum_ref[sl], low)
    for y in range(4):
        for s in range(2):
            for zz in range(2):
                row = zz * 32 + y * 8
                back[sl, y, s, :, zz * 128 : zz * 128 + 128] = total[row : row + 8, s * 128 : s * 128 + 128]


def smooth(angle, slab, c_ref, zlow, zhigh, ylow, yhigh, next_ref):
    lane = lax.broadcasted_iota(jnp.int32, (8, 128), 1)
    sub = lax.broadcasted_iota(jnp.int32, (8, 128), 0)
    has_zlow = (slab > 0).astype(f32)
    has_zhigh = (slab < 63).astype(f32)
    has_ylow = (angle > 0).astype(f32)
    has_yhigh = (angle < 3).astype(f32)

    def one(k, carry):
        c = c_ref[k]
        below, above = ylow[pl.ds(k, 1), :] * has_ylow, yhigh[pl.ds(k, 1), :] * has_yhigh
        half = (c[:, :128], c[:, 128:])
        deep = (zlow[k] * has_zlow + half[1], half[0] + zhigh[k] * has_zhigh)
        for zz in range(2):
            v = half[zz]
            at = slice(zz * 128, zz * 128 + 128)
            near = deep[zz]
            near += jnp.where(sub == 0, jnp.broadcast_to(below[:, at], (8, 128)), pltpu.roll(v, 1, 0))
            near += jnp.where(sub == 7, jnp.broadcast_to(above[:, at], (8, 128)), pltpu.roll(v, 7, 0))
            near += jnp.where(lane == 0, 0.0, pltpu.roll(v, 1, 1)) + jnp.where(lane == 127, 0.0, pltpu.roll(v, 127, 1))
            next_ref[k, :, at] = v - (STEP * SMOOTH) * (6.0 * v - near)
        return carry

    lax.fori_loop(0, 48, one, 0, unroll=4)


def main_kernel(
    stretch_ref, shift_ref, pick_v, sum_p, pick_p, sum_v, meas_ref, field0, c0_ref, harm_f, harm_t,
    out_ref, mout_ref,
    field1, c1_ref, next_ref, proj, sums, misfit, picked, contrib, split, back, got, fields, zlow, zhigh, ylow, yhigh, edges,
    send_sem, recv_sem,
):
    angle, x, z, half = position()
    slab = (x * 8 + z) * 2 + half
    mine = x * 2 + half
    block = (angle * 2 + half) * 4 + x
    a = stretch_ref[0]
    inv = stretch_ref[1]
    plane = [
        device(lax.rem(angle + k // 8, 4), lax.rem(x + k // 2, 4), z, lax.rem(half + k % 2, 2)) for k in range(1, 32)
    ]
    line = [device(angle, x, lax.rem(z + k, 8), half) for k in range(1, 8)]
    beyond = (angle, lax.rem(slab + 2 * half + 63, 64))
    partners = plane + line + [beyond]
    above = (angle, lax.rem(slab + 1, 64))
    below = (angle, lax.rem(slab + 63, 64))
    right = (lax.rem(angle + 1, 4), slab)
    left = (lax.rem(angle + 3, 4), slab)
    signal(partners)

    def halos(it, c_ref):
        base = it * 8
        edges[it, 0] = c_ref[:, 7, :]
        edges[it, 1] = c_ref[:, 0, :]
        send(c_ref.at[:, :, pl.ds(128, 128)], zlow.at[it], send_sem.at[base + 4], recv_sem.at[base + 4], above)
        send(c_ref.at[:, :, pl.ds(0, 128)], zhigh.at[it], send_sem.at[base + 5], recv_sem.at[base + 5], below)
        send(edges.at[it, 0], ylow.at[it], send_sem.at[base + 6], recv_sem.at[base + 6], right)
        send(edges.at[it, 1], yhigh.at[it], send_sem.at[base + 7], recv_sem.at[base + 7], left)

    def drain_halos(it, sems):
        base = it * 8
        drain(zlow.at[it], sems.at[base + 4])
        drain(zhigh.at[it], sems.at[base + 5])
        drain(ylow.at[it], sems.at[base + 6])
        drain(yhigh.at[it], sems.at[base + 7])

    for it in range(2):
        base = it * 8
        field = field0 if it == 0 else field1
        c_ref = c0_ref if it == 0 else c1_ref

        def project(sl, carry):
            project_slab(sl, a, inv, shift_ref, pick_v, field, picked, contrib)
            return carry

        if it == 0:
            lax.fori_loop(0, 4, project, 0)
            await_signals(partners)
            halos(0, c0_ref)
            lax.fori_loop(4, 8, project, 0)
        else:
            lax.fori_loop(0, 8, project, 0)
        total = jnp.zeros((128, 256), f32)
        for g in range(4):
            rows = slice(g * 384, (g + 1) * 384)
            for part in parts(contrib[rows], 3):
                total = total + hot(sum_p[:, rows], part)
        proj[it] = total.reshape(8, 16, 256)

        for k in (4, 3, 5, 2, 6, 1, 7):
            zz = lax.rem(z + k, 8)
            send(proj.at[it, zz], sums.at[it, k - 1], send_sem.at[base], recv_sem.at[base], line[k - 1])
        drain_halos(it, recv_sem)
        smooth(angle, slab, c_ref, zlow.at[it], zhigh.at[it], ylow.at[it], yhigh.at[it], next_ref)
        drain(sums.at[it], recv_sem.at[base])
        own = proj[it, z] - meas_ref[...]
        for k in range(7):
            own = own + sums[it, k]
        misfit[it, z] = own
        for k in (4, 3, 5, 2, 6, 1, 7):
            send(misfit.at[it, z], misfit.at[it, z], send_sem.at[base + 1], recv_sem.at[base + 1], line[k - 1])
        if it == 1:
            mout_ref[mine] = own
            for k in range(1, 8):
                target = device(angle, lax.rem(x + k // 2, 4), z, lax.rem(half + k % 2, 2))
                send(misfit.at[it, z], mout_ref.at[mine], send_sem.at[16], recv_sem.at[16], target)
        drain(misfit.at[it, pl.ds(0, 7)], recv_sem.at[base + 1])

        high, low = parts(misfit[it].reshape(128, 256), 2)
        split[:128] = high
        split[128:] = low

        def give(i, carry):
            xx, hh = lax.rem(x + lax.div(i, 2), 4), lax.rem(half + lax.rem(i, 2), 2)
            sl = xx * 2 + hh
            back_slab(sl, a, shift_ref, pick_p, sum_v, split, picked, contrib, back.at[it])
            for k in range(4):
                aa = lax.rem(angle + k, 4)
                send(back.at[it, sl, aa], got.at[it, block], send_sem.at[base + 2], recv_sem.at[base + 2], device(aa, xx, z, hh))
            return carry

        lax.fori_loop(1, 8, give, 0)
        back_slab(mine, a, shift_ref, pick_p, sum_v, split, picked, contrib, back.at[it])
        for k in range(1, 4):
            aa = lax.rem(angle + k, 4)
            send(back.at[it, mine, aa], got.at[it, block], send_sem.at[base + 2], recv_sem.at[base + 2], device(aa, x, z, half))
        got[it, block] = back[it, mine, angle]
        drain(got.at[it, pl.ds(0, 31)], recv_sem.at[base + 2])
        terms = got[it].reshape(512, 256)

        if it == 0:
            new = next_ref[...].reshape(384, 256) - STEP * dot(harm_t[...], terms)
            c1_ref[...] = new.reshape(48, 8, 256)
            fields[...] = dot(harm_f[...], new).reshape(32, 2, 8, 256)
            for k in range(1, 32):
                aa, xx, hh = lax.rem(angle + k // 8, 4), lax.rem(x + k // 2, 4), lax.rem(half + k % 2, 2)
                send(
                    fields.at[(aa * 2 + hh) * 4 + xx], field1.at[mine, angle],
                    send_sem.at[base + 3], recv_sem.at[base + 3], device(aa, xx, z, hh),
                )
            field1[mine, angle] = fields[block]
            halos(1, c1_ref)
            drain(got.at[it, pl.ds(0, 31)], recv_sem.at[base + 3])
        else:
            far = lax.rem(angle + 2, 4)
            beside = angle + 1 - 2 * lax.rem(angle, 2)
            groups = ((0, 16), (16, 16), (32, 13))

            def quarter(start, size, which):
                return out_ref.at[pl.ds(start, size), :, pl.ds(pl.multiple_of(which * 8, 8), 8), :]

            for g, (start, size) in enumerate(groups):
                rows = slice(start * 8, (start + size) * 8)
                new = next_ref[start : start + size].reshape(size * 8, 256) - STEP * dot(harm_t[rows, :], terms)
                new = new.reshape(size, 8, 256)
                for zz in range(2):
                    out_ref[start : start + size, zz, pl.ds(pl.multiple_of(angle * 8, 8), 8), :] = new[:, :, zz * 128 : zz * 128 + 128]
                piece = quarter(start, size, angle)
                send(piece, piece, send_sem.at[17 + g], recv_sem.at[17 + g], (far, slab))
                send(piece, piece, send_sem.at[20 + g], recv_sem.at[20 + g], (beside, slab))
            for g, (start, size) in enumerate(groups):
                piece = quarter(start, size, far)
                drain(piece, recv_sem.at[17 + g])
                send(piece, piece, send_sem.at[23 + g], recv_sem.at[23 + g], (beside, slab))
            for g, (start, size) in enumerate(groups):
                piece = quarter(start, size, angle)
                drain(piece, recv_sem.at[20 + g])
                drain(piece, recv_sem.at[23 + g])
                for first in (17, 20, 23):
                    drain(piece, send_sem.at[first + g])
            drain(mout_ref.at[pl.ds(0, 7)], recv_sem.at[16])
            drain(mout_ref.at[pl.ds(0, 7)], send_sem.at[16])

    for it in range(2):
        base = it * 8
        drain(sums.at[it], send_sem.at[base])
        drain(misfit.at[it, pl.ds(0, 7)], send_sem.at[base + 1])
        drain(got.at[it, pl.ds(0, 31)], send_sem.at[base + 2])
        if it == 0:
            drain(got.at[it, pl.ds(0, 31)], send_sem.at[base + 3])
        drain_halos(it, send_sem)


def main(*operands):
    return pl.pallas_call(
        main_kernel,
        out_shape=(jax.ShapeDtypeStruct((45, 2, 32, 128), f32), jax.ShapeDtypeStruct((8, 16, 256), f32)),
        in_specs=[SM] + [VM] * 10,
        out_specs=(VM, VM),
        scratch_shapes=[
            pltpu.VMEM((8, 4, 2, 8, 256), f32),
            pltpu.VMEM((48, 8, 256), f32),
            pltpu.VMEM((48, 8, 256), f32),
            pltpu.VMEM((2, 8, 16, 256), f32),
            pltpu.VMEM((2, 7, 16, 256), f32),
            pltpu.VMEM((2, 8, 16, 256), f32),
            pltpu.VMEM((TS, 256), f32),
            pltpu.VMEM((8 * TS, 256), f32),
            pltpu.VMEM((256, 256), bf16),
            pltpu.VMEM((2, 8, 4, 2, 8, 256), f32),
            pltpu.VMEM((2, 32, 2, 8, 256), f32),
            pltpu.VMEM((32, 2, 8, 256), f32),
            pltpu.VMEM((2, 48, 8, 128), f32),
            pltpu.VMEM((2, 48, 8, 128), f32),
            pltpu.VMEM((2, 48, 256), f32),
            pltpu.VMEM((2, 48, 256), f32),
            pltpu.VMEM((2, 2, 48, 256), f32),
            pltpu.SemaphoreType.DMA((26,)),
            pltpu.SemaphoreType.DMA((26,)),
        ],
        compiler_params=pltpu.CompilerParams(collective_id=1, has_side_effects=True, vmem_limit_bytes=LIMIT),
        name="main",
    )(*operands)


def pick(array, index, axis):
    return lax.dynamic_index_in_dim(array, index, axis, keepdims=False)


def per_device(coefficients, harmonics, stretch, measured, tile_pixel, tile_voxel, tile_shift, tile_count):
    angle, x, z, half = position()
    field, harm_got, packs, c_own = begin(coefficients, harmonics, tile_pixel, tile_voxel, tile_shift, tile_count, measured)

    slots = pick(packs[:, :8].reshape(8, 4, 2, 256), half, 2)[:, :3, :TS]
    pixel = slots[:, 0].astype(jnp.int32)
    voxel = slots[:, 1].astype(jnp.int32)
    pixel = lax.rem(lax.div(pixel, 4), 8) * 16 + lax.div(pixel, 32) * 4 + lax.rem(pixel, 4)
    count = 8 * TS

    def compare(ids, along, wrap):
        return jnp.where(ids == lax.rem(along, wrap), 1.0, 0.0).astype(bf16)

    pick_v = compare(voxel.reshape(count, 1), jnp.arange(192)[None, :], 64)
    pick_p = compare(pixel.reshape(count, 1), jnp.arange(256)[None, :], 128)
    sum_p = compare(pixel.reshape(1, count), jnp.arange(128)[:, None], 128)
    sum_v = compare(voxel[:, None, :], jnp.arange(64)[None, :, None], 64)
    shifts = jnp.broadcast_to(slots[:, 2].reshape(count, 1), (count, 128))
    a = pick(stretch, half, 0)
    stretch2 = jnp.stack([a, 1.0 / a])
    meas = pick(packs[:, 8:].reshape(8, 2, 8, 256), half, 1)
    meas = lax.dynamic_slice_in_dim(meas, 2 * x, 2, 1)
    meas = meas.reshape(8, 2, 2, 128).transpose(0, 2, 1, 3).reshape(16, 256)
    harm = harm_got.reshape(64, 128)[:, :48]
    eye = jnp.eye(8, dtype=f32)
    harm_f = (harm[:, None, :, None] * eye[None, :, None, :]).reshape(512, 384)
    harm_t = (harm.T[:, None, :, None] * eye[None, :, None, :]).reshape(384, 512)

    updated, mout = main(stretch2, shifts, pick_v, sum_p, pick_p, sum_v, meas, field, c_own, harm_f, harm_t)
    mout = pick(mout.reshape(4, 2, 8, 2, 2, 128), x * 2 + half, 2)
    misfit = mout.transpose(1, 0, 3, 2, 4).reshape(2, 8, 256)
    return updated, misfit


def solution(mesh):
    in_specs = (
        P(None, "slab", None, None),
        P("angle", None, None),
        P("angle"),
        P("angle", None, "slab"),
        P("angle", "slab"),
        P("angle", "slab"),
        P("angle", "slab"),
        P("angle", "slab"),
    )
    out_specs = (P(None, "slab", None, None), P("angle", None, "slab"))
    return jax.shard_map(per_device, mesh=mesh, in_specs=in_specs, out_specs=out_specs, check_vma=False)
```

```python
import jax
import jax.numpy as jnp
from jax import lax
from jax.experimental import pallas as pl
from jax.experimental.pallas import tpu as pltpu
from jax.sharding import PartitionSpec as P

f32 = jnp.float32
bf16 = jnp.bfloat16
MESH = pl.DeviceIdType.MESH
STEP = 0.003
SMOOTH = 6.0
FAR = 1.0e6
TS = 192
CHUNK = 48
TAKE = lax.GatherDimensionNumbers(
    offset_dims=(), collapsed_slice_dims=(1,), start_index_map=(1,), operand_batching_dims=(0,), start_indices_batching_dims=(0,)
)

VM = pl.BlockSpec(memory_space=pltpu.VMEM)
SM = pl.BlockSpec(memory_space=pltpu.SMEM)
LIMIT = 48 * 2**20


def position():
    angle = lax.axis_index("angle")
    slab = lax.axis_index("slab")
    return angle, lax.div(slab, 16), lax.rem(lax.div(slab, 2), 8), lax.rem(slab, 2)


def device(angle, x, z, half):
    return (angle, (x * 8 + z) * 2 + half)


def signal(partners):
    barrier = pltpu.get_barrier_semaphore()
    for partner in partners:
        pl.semaphore_signal(barrier, inc=1, device_id=partner, device_id_type=MESH)


def await_signals(partners):
    pl.semaphore_wait(pltpu.get_barrier_semaphore(), len(partners))


def send(src, dst, send_sem, recv_sem, target):
    pltpu.make_async_remote_copy(
        src_ref=src, dst_ref=dst, send_sem=send_sem, recv_sem=recv_sem, device_id=target, device_id_type=MESH
    ).start()


def drain(like, sem):
    pltpu.make_async_copy(like, like, sem).wait()


def dot(a, b):
    return jnp.dot(a, b, preferred_element_type=f32, precision=lax.Precision.HIGHEST)


def hot(a, b):
    return jnp.dot(a, b, preferred_element_type=f32)


def parts(value, count):
    found = []
    for _ in range(count - 1):
        part = value.astype(bf16)
        found.append(part)
        value = value - part.astype(f32)
    return found + [value.astype(bf16)]


def take(values, lanes):
    return lax.gather(values, lanes[..., None], TAKE, slice_sizes=(1, 1), mode=lax.GatherScatterMode.PROMISE_IN_BOUNDS)


def project_slab(i, a, inv, shift_ref, pick_ref, field, picked, contrib):
    rows = [
        jnp.concatenate([field[i, y, s, :, zz * 128 : zz * 128 + 128] for s in range(2)], axis=1)
        for zz in range(2)
        for y in range(4)
    ]
    split = jnp.concatenate(parts(jnp.concatenate(rows, axis=0), 3), axis=0)
    picked[...] = hot(pick_ref[pl.ds(pl.multiple_of(i * TS, TS), TS), :], split)
    lane = lax.broadcasted_iota(jnp.int32, (CHUNK, 128), 1).astype(f32)
    for c in range(TS // CHUNK):
        at = pl.ds(pl.multiple_of(i * TS + c * CHUNK, 16), CHUNK)
        u = lane - shift_ref[at, :]
        v0 = jnp.floor((u - 1.0) * inv) + 1.0
        t0 = u - a * v0
        first = v0.astype(jnp.int32)
        taps = (1.0 - t0, 1.0 - jnp.abs(t0 - a), 1.0 + t0 - 2.0 * a, 1.0 + t0 - 3.0 * a)
        lanes, weights = [], []
        for k in range(4):
            v = first + k
            inside = v & 127
            lanes.append(inside)
            weights.append(jnp.where(v == inside, jnp.maximum(taps[k], 0.0), 0.0))
        for s in range(2):
            f = picked[c * CHUNK : (c + 1) * CHUNK, s * 128 : s * 128 + 128]
            terms = [take(f, lanes[k]) * weights[k] for k in range(4)]
            contrib[at, s * 128 : s * 128 + 128] = (terms[0] + terms[1]) + (terms[2] + terms[3])


def back_slab(i, a, shift_ref, pick_ref, sum_ref, split, picked, contrib, back):
    picked[...] = hot(pick_ref[pl.ds(pl.multiple_of(i * TS, TS), TS), :], split[...])
    lane = lax.broadcasted_iota(jnp.int32, (CHUNK, 128), 1).astype(f32)
    for c in range(TS // CHUNK):
        at = slice(c * CHUNK, (c + 1) * CHUNK)
        t = shift_ref[pl.ds(pl.multiple_of(i * TS + c * CHUNK, 16), CHUNK), :] + a * lane
        p0 = jnp.floor(t)
        w1 = t - p0
        w0 = jnp.where(p0 <= 127.0, 1.0 - w1, 0.0)
        w1 = jnp.where(p0 <= 126.0, w1, 0.0)
        first = p0.astype(jnp.int32)
        lane0, lane1 = first & 127, (first + 1) & 127
        for s in range(2):
            m = picked[at, s * 128 : s * 128 + 128]
            contrib[at, s * 128 : s * 128 + 128] = take(m, lane0) * w0 + take(m, lane1) * w1
    high, low = parts(contrib[:TS], 2)
    total = hot(sum_ref[i], high) + hot(sum_ref[i], low)
    for y in range(4):
        for s in range(2):
            for zz in range(2):
                row = zz * 32 + y * 8
                back[i, y, s, :, zz * 128 : zz * 128 + 128] = total[row : row + 8, s * 128 : s * 128 + 128]


def smooth(angle, slab, c_ref, zlow, zhigh, ylow, yhigh, next_ref):
    lane = lax.broadcasted_iota(jnp.int32, (8, 128), 1)
    sub = lax.broadcasted_iota(jnp.int32, (8, 128), 0)
    has_zlow = (slab > 0).astype(f32)
    has_zhigh = (slab < 63).astype(f32)
    has_ylow = (angle > 0).astype(f32)
    has_yhigh = (angle < 3).astype(f32)

    def one(k, carry):
        c = c_ref[k]
        below, above = ylow[pl.ds(k, 1), :] * has_ylow, yhigh[pl.ds(k, 1), :] * has_yhigh
        half = (c[:, :128], c[:, 128:])
        deep = (zlow[k] * has_zlow + half[1], half[0] + zhigh[k] * has_zhigh)
        for zz in range(2):
            v = half[zz]
            at = slice(zz * 128, zz * 128 + 128)
            near = deep[zz]
            near += jnp.where(sub == 0, jnp.broadcast_to(below[:, at], (8, 128)), pltpu.roll(v, 1, 0))
            near += jnp.where(sub == 7, jnp.broadcast_to(above[:, at], (8, 128)), pltpu.roll(v, 7, 0))
            near += jnp.where(lane == 0, 0.0, pltpu.roll(v, 1, 1)) + jnp.where(lane == 127, 0.0, pltpu.roll(v, 127, 1))
            next_ref[k, :, at] = v - (STEP * SMOOTH) * (6.0 * v - near)
        return carry

    lax.fori_loop(0, 48, one, 0, unroll=4)


def prepare_slots(packs, half, pick_v, pick_p, sum_v, sum_p, shift_b):
    row = lax.broadcasted_iota(jnp.int32, (8, 640), 0)
    lane = lax.broadcasted_iota(jnp.int32, (8, 640), 1)
    spread = ((lane < 256) & (row == 0)) | ((lane >= 256) & (lane < 512) & (row == 1)) | ((lane >= 512) & (row >= 2) & (row <= 4))
    spread = jnp.where(spread, 1.0, 0.0).astype(bf16)
    id_v = lax.rem(lax.broadcasted_iota(jnp.int32, (TS, 192), 1), 64).astype(f32)
    id_p = lax.rem(lax.broadcasted_iota(jnp.int32, (TS, 256), 1), 128).astype(f32)
    sub_v = lax.broadcasted_iota(jnp.int32, (64, TS), 0).astype(f32)
    sub_p = lax.broadcasted_iota(jnp.int32, (128, 2 * TS), 0).astype(f32)

    def hit(ids, along):
        return jnp.where(ids == along, 1.0, 0.0).astype(bf16)

    rows_p = []
    for i in range(8):
        pixel = packs[i, pl.ds(half, 1), :]
        voxel = packs[i, pl.ds(2 + half, 1), :]
        shift = packs[i, pl.ds(4 + half, 1), :]
        split = [part.astype(f32) for part in parts(shift, 3)]
        rows = jnp.concatenate([voxel, pixel] + split + [jnp.zeros((3, 256), f32)], axis=0)
        wide = hot(rows.T.astype(bf16)[:TS], spread)
        at = slice(i * TS, (i + 1) * TS)
        pick_v[at, :] = hit(wide[:, :192], id_v)
        pick_p[at, :] = hit(wide[:, 256:512], id_p)
        shift_b[at, :] = wide[:, 512:640]
        sum_v[i] = hit(voxel[:, :TS], sub_v)
        rows_p.append(pixel[:, :TS])
    for g in range(4):
        sum_p[:, g * 384 : (g + 1) * 384] = hit(jnp.concatenate(rows_p[2 * g : 2 * g + 2], axis=1), sub_p)


def prepare_harmonics(harm_all, harm_f, harm_t):
    harm = harm_all[...].reshape(64, 128)

    def spread(rows, columns, along):
        big = lax.broadcasted_iota(jnp.int32, (rows, columns), along)
        small = lax.broadcasted_iota(jnp.int32, (rows, columns), 1 - along)
        return jnp.where(lax.div(big, 8) == small, 1.0, 0.0)

    def diagonal(rows, columns):
        r = lax.broadcasted_iota(jnp.int32, (rows, columns), 0)
        c = lax.broadcasted_iota(jnp.int32, (rows, columns), 1)
        return lax.rem(r, 8) == lax.rem(c, 8)

    wide = dot(harm, spread(128, 384, 1))
    harm_f[...] = jnp.where(diagonal(512, 384), dot(spread(512, 64, 0), wide), 0.0)
    wide = dot(harm.T, spread(64, 512, 1))
    full = jnp.where(diagonal(384, 512), dot(spread(384, 128, 0), wide), 0.0)
    high, low = parts(full, 2)
    harm_t[:, :512] = high
    harm_t[:, 512:1024] = high
    harm_t[:, 1024:] = low


SEM_PACK, SEM_HARM, SEM_FIELD, SEM_SUM, SEM_ALL, SEM_BACK, SEM_HALO, SEM_MIS, SEM_FAR, SEM_NEAR, SEM_PASS = (
    0, 1, 2, 18, 20, 22, 24, 32, 33, 36, 39,
)
SEMS = 42
FAR_FIRST = (4, 3, 5, 2, 6, 1, 7)


def kernel(
    c_hbm, harm_hbm, stretch_hbm, meas_hbm, pix_hbm, vox_hbm, shift_hbm, count_hbm,
    out_ref, mout_ref,
    c_all, harm_v, harm_s, stretch_s, meas_v, pix_v, vox_v, shift_v, count_v,
    pack, packs, blocks, field0, field1, harm_all, harm_f, harm_t, pick_v, pick_p, sum_v, sum_p, shift_b, meas_own,
    c0_ref, c1_ref, next_ref, proj, sums, misfit, picked, contrib, split, back, got, fields, zlow, zhigh, ylow, yhigh, edges,
    send_sem, recv_sem, load_sem,
):
    angle, x, z, half = position()
    slab = (x * 8 + z) * 2 + half
    mine = x * 2 + half
    block = (angle * 2 + half) * 4 + x
    plane = [
        device(lax.rem(angle + k // 8, 4), lax.rem(x + k // 2, 4), z, lax.rem(half + k % 2, 2)) for k in range(1, 32)
    ]
    line = [device(angle, x, lax.rem(z + k, 8), half) for k in range(1, 8)]
    beyond = (angle, lax.rem(slab + 2 * half + 63, 64))
    partners = plane + line + [beyond]
    above = (angle, lax.rem(slab + 1, 64))
    below = (angle, lax.rem(slab + 63, 64))
    right = (lax.rem(angle + 1, 4), slab)
    left = (lax.rem(angle + 3, 4), slab)
    back_of = [((4 - i // 2) % 4) * 2 + i % 2 for i in range(8)]

    loads = [
        pltpu.make_async_copy(src, dst, load_sem.at[n])
        for n, (src, dst) in enumerate(
            [
                (c_hbm, c_all), (harm_hbm, harm_s), (harm_hbm, harm_v), (pix_hbm, pix_v), (vox_hbm, vox_v),
                (shift_hbm, shift_v), (count_hbm, count_v), (meas_hbm, meas_v), (stretch_hbm, stretch_s),
            ]
        )
    ]
    for load in loads:
        load.start()
    signal(partners)
    for load in loads:
        load.wait()

    pixel = pix_v[...]
    pixel = lax.rem(lax.div(pixel, 4), 8) * 16 + lax.div(pixel, 32) * 4 + lax.rem(pixel, 4)
    valid = lax.broadcasted_iota(jnp.int32, (2, TS), 1) < count_v[...]
    pack[...] = jnp.zeros_like(pack)
    pack[0:2, :TS] = pixel.astype(f32)
    pack[2:4, :TS] = vox_v[...].astype(f32)
    pack[4:6, :TS] = jnp.where(valid, shift_v[...], FAR)
    pack[8:16] = meas_v[0]
    pack[16:24] = meas_v[1]
    packs[0] = pack[...]
    harm_all[angle] = jnp.zeros((16, 128), f32)
    harm_all[angle, 0:8, 0:45] = harm_v[0]
    harm_all[angle, 8:16, 0:45] = harm_v[1]
    quarter_y = pl.ds(pl.multiple_of(angle * 8, 8), 8)
    c0_ref[:45, :, 0:128] = c_all[:, 0, quarter_y, :]
    c0_ref[:45, :, 128:256] = c_all[:, 1, quarter_y, :]
    c0_ref[45:] = jnp.zeros((3, 8, 256), f32)

    def first_fields(which, segments, dest):
        for s in range(2):
            for zz in range(2):
                total = [None] * 4
                for k in range(45):
                    h = harm_s[which, segments * 2 + s, k]
                    for y in range(4):
                        term = c_all[k, zz, y * 8 : y * 8 + 8, :] * h
                        total[y] = term if k == 0 else total[y] + term
                for y in range(4):
                    dest[y, s, :, zz * 128 : zz * 128 + 128] = total[y]

    def first_block(i, carry):
        first_fields(lax.rem(half + lax.rem(i, 2), 2), lax.rem(x + lax.div(i, 2), 4), blocks.at[i])
        return carry

    lax.fori_loop(0, 8, first_block, 0)
    await_signals(partners)
    peers = [device(angle, lax.rem(x + i // 2, 4), z, lax.rem(half + i % 2, 2)) for i in range(8)]
    for i in range(1, 8):
        send(pack, packs.at[back_of[i]], send_sem.at[SEM_PACK], recv_sem.at[SEM_PACK], peers[i])
    for i in range(1, 8):
        send(
            blocks.at[i], field0.at[back_of[i]], send_sem.at[SEM_FIELD], recv_sem.at[SEM_FIELD + back_of[i]], peers[i]
        )
    for k in range(1, 4):
        target = device(lax.rem(angle + k, 4), x, z, half)
        send(harm_all.at[angle], harm_all.at[angle], send_sem.at[SEM_HARM], recv_sem.at[SEM_HARM], target)

    def halos(it, c_ref):
        at = SEM_HALO + it * 4
        edges[it, 0] = c_ref[:, 7, :]
        edges[it, 1] = c_ref[:, 0, :]
        send(c_ref.at[:, :, pl.ds(128, 128)], zlow.at[it], send_sem.at[at], recv_sem.at[at], above)
        send(c_ref.at[:, :, pl.ds(0, 128)], zhigh.at[it], send_sem.at[at + 1], recv_sem.at[at + 1], below)
        send(edges.at[it, 0], ylow.at[it], send_sem.at[at + 2], recv_sem.at[at + 2], right)
        send(edges.at[it, 1], yhigh.at[it], send_sem.at[at + 3], recv_sem.at[at + 3], left)

    def drain_halos(it, sems):
        for n, ref in enumerate((zlow, zhigh, ylow, yhigh)):
            drain(ref.at[it], sems.at[SEM_HALO + it * 4 + n])

    halos(0, c0_ref)
    field0[0] = blocks[0]
    a = stretch_s[half]
    inv = 1.0 / jnp.full((8, 128), a, f32)[0:1, :]
    drain(packs.at[pl.ds(0, 7)], recv_sem.at[SEM_PACK])
    prepare_slots(packs, half, pick_v, pick_p, sum_v, sum_p, shift_b)
    for n in range(8):
        i = lax.rem(n // 2 - x + 4, 4) * 2 + lax.rem(n % 2 - half + 2, 2)
        for s in range(2):
            line_of = packs[i, pl.ds(8 + half * 8 + x * 2 + s, 1), :]
            for tile in range(2):
                row = n * 2 + tile
                meas_own[row : row + 1, s * 128 : s * 128 + 128] = line_of[:, tile * 128 : tile * 128 + 128]

    for it in range(2):
        field = field0 if it == 0 else field1
        c_ref = c0_ref if it == 0 else c1_ref
        sem_field = SEM_FIELD + it * 8

        def project(i, carry):
            project_slab(i, a, inv, shift_b, pick_v, field, picked, contrib)

            @pl.when(i < 7)
            def _():
                drain(field.at[i + 1], recv_sem.at[sem_field + i + 1])

            return carry

        lax.fori_loop(0, 8, project, 0)
        total = jnp.zeros((128, 256), f32)
        for g in range(4):
            rows = slice(g * 384, (g + 1) * 384)
            for part in parts(contrib[rows], 3):
                total = total + hot(sum_p[:, rows], part)
        proj[it] = total.reshape(8, 16, 256)

        for k in FAR_FIRST:
            zz = lax.rem(z + k, 8)
            send(proj.at[it, zz], sums.at[it, k - 1], send_sem.at[SEM_SUM + it], recv_sem.at[SEM_SUM + it], line[k - 1])
        drain_halos(it, recv_sem)
        smooth(angle, slab, c_ref, zlow.at[it], zhigh.at[it], ylow.at[it], yhigh.at[it], next_ref)
        drain(sums.at[it], recv_sem.at[SEM_SUM + it])
        own = proj[it, z] - meas_own[...]
        for k in range(7):
            own = own + sums[it, k]
        misfit[it, z] = own
        for k in FAR_FIRST:
            send(misfit.at[it, z], misfit.at[it, z], send_sem.at[SEM_ALL + it], recv_sem.at[SEM_ALL + it], line[k - 1])
        if it == 0:
            drain(harm_all.at[pl.ds(0, 3)], recv_sem.at[SEM_HARM])
            prepare_harmonics(harm_all, harm_f, harm_t)
        else:
            mout_ref[mine] = own
            for i in range(1, 8):
                send(misfit.at[it, z], mout_ref.at[mine], send_sem.at[SEM_MIS], recv_sem.at[SEM_MIS], peers[i])
        drain(misfit.at[it, pl.ds(0, 7)], recv_sem.at[SEM_ALL + it])

        high, low = parts(misfit[it].reshape(128, 256), 2)
        split[:128] = high
        split[128:] = low

        def give(i, carry):
            xx, hh = lax.rem(x + lax.div(i, 2), 4), lax.rem(half + lax.rem(i, 2), 2)
            back_slab(i, a, shift_b, pick_p, sum_v, split, picked, contrib, back.at[it])
            for k in range(4):
                aa = lax.rem(angle + k, 4)
                send(
                    back.at[it, i, aa], got.at[it, block],
                    send_sem.at[SEM_BACK + it], recv_sem.at[SEM_BACK + it], device(aa, xx, z, hh),
                )
            return carry

        lax.fori_loop(1, 8, give, 0)
        back_slab(0, a, shift_b, pick_p, sum_v, split, picked, contrib, back.at[it])
        for k in range(1, 4):
            aa = lax.rem(angle + k, 4)
            send(
                back.at[it, 0, aa], got.at[it, block],
                send_sem.at[SEM_BACK + it], recv_sem.at[SEM_BACK + it], device(aa, x, z, half),
            )
        got[it, block] = back[it, 0, angle]
        drain(got.at[it, pl.ds(0, 31)], recv_sem.at[SEM_BACK + it])
        high, low = parts(got[it].reshape(512, 256), 2)
        terms = jnp.concatenate([high, low, high], axis=0)

        if it == 0:
            new = next_ref[...].reshape(384, 256) - STEP * hot(harm_t[...], terms)
            c1_ref[...] = new.reshape(48, 8, 256)
            fields[...] = dot(harm_f[...], new).reshape(32, 2, 8, 256)
            for k in sorted(range(1, 32), key=lambda k: (k % 8, k)):
                aa, xx, hh = lax.rem(angle + k // 8, 4), lax.rem(x + k % 8 // 2, 4), lax.rem(half + k % 2, 2)
                to = back_of[k % 8]
                send(
                    fields.at[(aa * 2 + hh) * 4 + xx], field1.at[to, angle],
                    send_sem.at[SEM_FIELD + 8], recv_sem.at[SEM_FIELD + 8 + to], device(aa, xx, z, hh),
                )
            field1[0, angle] = fields[block]
            halos(1, c1_ref)
            drain(field1.at[0, pl.ds(0, 3)], recv_sem.at[SEM_FIELD + 8])
        else:
            far = lax.rem(angle + 2, 4)
            beside = angle + 1 - 2 * lax.rem(angle, 2)
            groups = ((0, 16), (16, 16), (32, 13))

            def quarter(start, size, which):
                return out_ref.at[pl.ds(start, size), :, pl.ds(pl.multiple_of(which * 8, 8), 8), :]

            for g, (start, size) in enumerate(groups):
                rows = slice(start * 8, (start + 16) * 8)
                new = next_ref[start : start + 16].reshape(128, 256) - STEP * hot(harm_t[rows, :], terms)
                new = new.reshape(16, 8, 256)[:size]
                for zz in range(2):
                    out_ref[start : start + size, zz, quarter_y, :] = new[:, :, zz * 128 : zz * 128 + 128]
                piece = quarter(start, size, angle)
                send(piece, piece, send_sem.at[SEM_FAR + g], recv_sem.at[SEM_FAR + g], (far, slab))
                send(piece, piece, send_sem.at[SEM_NEAR + g], recv_sem.at[SEM_NEAR + g], (beside, slab))
            for g, (start, size) in enumerate(groups):
                piece = quarter(start, size, far)
                drain(piece, recv_sem.at[SEM_FAR + g])
                send(piece, piece, send_sem.at[SEM_PASS + g], recv_sem.at[SEM_PASS + g], (beside, slab))
            for g, (start, size) in enumerate(groups):
                piece = quarter(start, size, angle)
                drain(piece, recv_sem.at[SEM_NEAR + g])
                drain(piece, recv_sem.at[SEM_PASS + g])
                for first in (SEM_FAR, SEM_NEAR, SEM_PASS):
                    drain(piece, send_sem.at[first + g])
            drain(mout_ref.at[pl.ds(0, 7)], recv_sem.at[SEM_MIS])
            drain(mout_ref.at[pl.ds(0, 7)], send_sem.at[SEM_MIS])

    drain(packs.at[pl.ds(0, 7)], send_sem.at[SEM_PACK])
    drain(harm_all.at[pl.ds(0, 3)], send_sem.at[SEM_HARM])
    drain(field0.at[pl.ds(0, 7)], send_sem.at[SEM_FIELD])
    drain(got.at[0, pl.ds(0, 31)], send_sem.at[SEM_FIELD + 8])
    for it in range(2):
        drain(sums.at[it], send_sem.at[SEM_SUM + it])
        drain(misfit.at[it, pl.ds(0, 7)], send_sem.at[SEM_ALL + it])
        drain(got.at[it, pl.ds(0, 31)], send_sem.at[SEM_BACK + it])
        drain_halos(it, send_sem)


def per_device(coefficients, harmonics, stretch, measured, tile_pixel, tile_voxel, tile_shift, tile_count):
    angle, x, z, half = position()
    operands = (coefficients, harmonics, stretch, measured, tile_pixel, tile_voxel, tile_shift, tile_count)
    scratch = [
        pltpu.VMEM((45, 2, 32, 128), f32),
        pltpu.VMEM((2, 8, 45), f32),
        pltpu.SMEM((2, 8, 45), f32),
        pltpu.SMEM((2,), f32),
        pltpu.VMEM((2, 8, 256), f32),
        pltpu.VMEM((2, TS), jnp.int32),
        pltpu.VMEM((2, TS), jnp.int32),
        pltpu.VMEM((2, TS), f32),
        pltpu.VMEM((2, 1), jnp.int32),
        pltpu.VMEM((24, 256), f32),
        pltpu.VMEM((8, 24, 256), f32),
        pltpu.VMEM((8, 4, 2, 8, 256), f32),
        pltpu.VMEM((8, 4, 2, 8, 256), f32),
        pltpu.VMEM((8, 4, 2, 8, 256), f32),
        pltpu.VMEM((4, 16, 128), f32),
        pltpu.VMEM((512, 384), f32),
        pltpu.VMEM((384, 1536), bf16),
        pltpu.VMEM((8 * TS, 192), bf16),
        pltpu.VMEM((8 * TS, 256), bf16),
        pltpu.VMEM((8, 64, TS), bf16),
        pltpu.VMEM((128, 8 * TS), bf16),
        pltpu.VMEM((8 * TS, 128), f32),
        pltpu.VMEM((16, 256), f32),
        pltpu.VMEM((48, 8, 256), f32),
        pltpu.VMEM((48, 8, 256), f32),
        pltpu.VMEM((48, 8, 256), f32),
        pltpu.VMEM((2, 8, 16, 256), f32),
        pltpu.VMEM((2, 7, 16, 256), f32),
        pltpu.VMEM((2, 8, 16, 256), f32),
        pltpu.VMEM((TS, 256), f32),
        pltpu.VMEM((8 * TS, 256), f32),
        pltpu.VMEM((256, 256), bf16),
        pltpu.VMEM((2, 8, 4, 2, 8, 256), f32),
        pltpu.VMEM((2, 32, 2, 8, 256), f32),
        pltpu.VMEM((32, 2, 8, 256), f32),
        pltpu.VMEM((2, 48, 8, 128), f32),
        pltpu.VMEM((2, 48, 8, 128), f32),
        pltpu.VMEM((2, 48, 256), f32),
        pltpu.VMEM((2, 48, 256), f32),
        pltpu.VMEM((2, 2, 48, 256), f32),
        pltpu.SemaphoreType.DMA((SEMS,)),
        pltpu.SemaphoreType.DMA((SEMS,)),
        pltpu.SemaphoreType.DMA((9,)),
    ]
    updated, mout = pl.pallas_call(
        kernel,
        out_shape=(jax.ShapeDtypeStruct((45, 2, 32, 128), f32), jax.ShapeDtypeStruct((8, 16, 256), f32)),
        in_specs=[pl.BlockSpec(memory_space=pl.ANY)] * 8,
        out_specs=(VM, VM),
        scratch_shapes=scratch,
        compiler_params=pltpu.CompilerParams(collective_id=0, has_side_effects=True, vmem_limit_bytes=LIMIT),
        name="tomography",
    )(*operands)
    mout = lax.dynamic_index_in_dim(mout.reshape(4, 2, 8, 2, 2, 128), x * 2 + half, 2, keepdims=False)
    misfit = mout.transpose(1, 0, 3, 2, 4).reshape(2, 8, 256)
    return updated, misfit


def solution(mesh):
    in_specs = (
        P(None, "slab", None, None),
        P("angle", None, None),
        P("angle"),
        P("angle", None, "slab"),
        P("angle", "slab"),
        P("angle", "slab"),
        P("angle", "slab"),
        P("angle", "slab"),
    )
    out_specs = (P(None, "slab", None, None), P("angle", None, "slab"))
    return jax.shard_map(per_device, mesh=mesh, in_specs=in_specs, out_specs=out_specs, check_vma=False)
```

```python
import jax
import jax.numpy as jnp
from jax import lax
from jax.experimental import pallas as pl
from jax.experimental.pallas import tpu as pltpu
from jax.sharding import PartitionSpec as P

f32 = jnp.float32
bf16 = jnp.bfloat16
MESH = pl.DeviceIdType.MESH
STEP = 0.003
SMOOTH = 6.0
FAR = 128.0
FIX = 23
TS = 192
CHUNK = 48
TAKE = lax.GatherDimensionNumbers(
    offset_dims=(), collapsed_slice_dims=(1,), start_index_map=(1,), operand_batching_dims=(0,), start_indices_batching_dims=(0,)
)

VM = pl.BlockSpec(memory_space=pltpu.VMEM)
SM = pl.BlockSpec(memory_space=pltpu.SMEM)
LIMIT = 56 * 2**20


def position():
    angle = lax.axis_index("angle")
    slab = lax.axis_index("slab")
    return angle, lax.div(slab, 16), lax.rem(lax.div(slab, 2), 8), lax.rem(slab, 2)


def device(angle, x, z, half):
    return (angle, (x * 8 + z) * 2 + half)


def signal(partners):
    barrier = pltpu.get_barrier_semaphore()
    for partner in partners:
        pl.semaphore_signal(barrier, inc=1, device_id=partner, device_id_type=MESH)


def await_signals(partners):
    pl.semaphore_wait(pltpu.get_barrier_semaphore(), len(partners))


def send(src, dst, send_sem, recv_sem, target):
    pltpu.make_async_remote_copy(
        src_ref=src, dst_ref=dst, send_sem=send_sem, recv_sem=recv_sem, device_id=target, device_id_type=MESH
    ).start()


def drain(like, sem):
    pltpu.make_async_copy(like, like, sem).wait()


def dot(a, b):
    return jnp.dot(a, b, preferred_element_type=f32, precision=lax.Precision.HIGHEST)


def hot(a, b):
    return jnp.dot(a, b, preferred_element_type=f32)


def parts(value, count):
    found = []
    for _ in range(count - 1):
        part = value.astype(bf16)
        found.append(part)
        value = value - part.astype(f32)
    return found + [value.astype(bf16)]


def take(values, lanes):
    return lax.gather(values, lanes[..., None], TAKE, slice_sizes=(1, 1), mode=lax.GatherScatterMode.PROMISE_IN_BOUNDS)


def project_pick(i, pick_ref, field, picked):
    rows = [
        jnp.concatenate([field[i, y, s, :, zz * 128 : zz * 128 + 128] for s in range(2)], axis=1)
        for zz in range(2)
        for y in range(4)
    ]
    rows = jnp.concatenate(rows, axis=0)
    ahead = [pltpu.roll(rows[:, s * 128 : s * 128 + 128], 127, 1) for s in range(2)]
    split = jnp.concatenate(parts(jnp.concatenate([rows] + ahead, axis=1), 3), axis=0)
    picked[...] = hot(pick_ref[pl.ds(pl.multiple_of(i * TS, TS), TS), :], split)


def project_slots(i, stretch, shift_ref, picked, contrib):
    one = 1 << FIX
    scale = 1.0 / one
    lane = lax.broadcasted_iota(jnp.int32, (1, 128), 1)
    step = (jnp.full((1, 128), stretch, f32) * one + 0.5).astype(jnp.int32)
    inverse = 1.0 / step.astype(f32)
    steps = step * lane

    def first_of(distance):
        first = jnp.ceil(distance.astype(f32) * inverse - 2.0e-4).astype(jnp.int32)
        first = jnp.where(first * step < distance, first + 1, first)
        return jnp.maximum(first, 0)

    for c in range(TS // CHUNK):
        at = slice(c * CHUNK, (c + 1) * CHUNK)
        start = (shift_ref[pl.ds(pl.multiple_of(i * TS + c * CHUNK, 16), CHUNK), :] * one + 0.5).astype(jnp.int32)
        here = start + steps
        after = here + step
        w1 = (here & (one - 1)).astype(f32) * scale
        w0 = 1.0 - w1
        both = (lax.shift_right_arithmetic(here, FIX) == lax.shift_right_arithmetic(after, FIX)) & (lane < 127)
        next1 = (after & (one - 1)).astype(f32) * scale
        next0 = jnp.where(both, 1.0 - next1, 0.0)
        next1 = jnp.where(both, next1, 0.0)
        distance = (lane << FIX) - start
        first0, first1 = first_of(distance), first_of(distance - one)
        has0 = (first0 <= 127) & (distance > -one)
        has1 = (first1 <= 127) & (distance > 0)
        first0, first1 = first0 & 127, first1 & 127
        for s in range(2):
            f = picked[at, s * 128 : s * 128 + 128]
            g = picked[at, 256 + s * 128 : 256 + s * 128 + 128]
            low = jnp.where(has0, take(w0 * f + next0 * g, first0), 0.0)
            high = jnp.where(has1, take(w1 * f + next1 * g, first1), 0.0)
            contrib[at, s * 128 : s * 128 + 128] = low + high


def project_sum(i, sum_ref, contrib, total):
    for part in parts(contrib[...], 3):
        total[...] += hot(sum_ref[i], part)


def project_all(stretch, shift_ref, pick_ref, sum_ref, field, arrived, rows, added, total):
    total[...] = jnp.zeros_like(total)

    def step(i, odd, pick_next=True, sum_last=True):
        if pick_next:
            arrived(i + 1)
            project_pick(i + 1, pick_ref, field, rows[1 - odd])
        project_slots(i, stretch, shift_ref, rows[odd], added[odd])
        if sum_last:
            project_sum(i - 1, sum_ref, added[1 - odd], total)

    def pair(p, carry):
        step(2 * p + 1, 1)
        step(2 * p + 2, 0)
        return carry

    project_pick(0, pick_ref, field, rows[0])
    step(0, 0, sum_last=False)
    lax.fori_loop(0, 3, pair, 0)
    step(7, 1, pick_next=False)
    project_sum(7, sum_ref, added[1], total)


def back_pick(i, pick_ref, split, picked):
    picked[:, :256] = hot(pick_ref[pl.ds(pl.multiple_of(i * TS, TS), TS), :], split[...])


def back_slots(i, stretch, shift_ref, picked, contrib):
    lane = lax.broadcasted_iota(jnp.int32, (1, 128), 1).astype(f32) * stretch
    for c in range(TS // CHUNK):
        at = slice(c * CHUNK, (c + 1) * CHUNK)
        t = shift_ref[pl.ds(pl.multiple_of(i * TS + c * CHUNK, 16), CHUNK), :] + lane
        p0 = jnp.floor(t)
        w1 = t - p0
        w0 = jnp.where(p0 <= 127.0, 1.0 - w1, 0.0)
        w1 = jnp.where(p0 <= 126.0, w1, 0.0)
        first = p0.astype(jnp.int32)
        lane0, lane1 = first & 127, (first + 1) & 127
        for s in range(2):
            m = picked[at, s * 128 : s * 128 + 128]
            contrib[at, s * 128 : s * 128 + 128] = take(m, lane0) * w0 + take(m, lane1) * w1


def back_sum(i, sum_ref, contrib, back):
    high, low = parts(contrib[...], 2)
    total = hot(sum_ref[i], high) + hot(sum_ref[i], low)
    for y in range(4):
        for s in range(2):
            for zz in range(2):
                row = zz * 32 + y * 8
                back[i, y, s, :, zz * 128 : zz * 128 + 128] = total[row : row + 8, s * 128 : s * 128 + 128]


def back_all(stretch, shift_ref, pick_ref, sum_ref, split, give, rows, added, back):
    def step(i, odd, pick_next=True, sum_last=True):
        if pick_next:
            back_pick(lax.rem(i + 1, 8), pick_ref, split, rows[1 - odd])
        back_slots(lax.rem(i, 8), stretch, shift_ref, rows[odd], added[odd])
        if sum_last:
            back_sum(i - 1, sum_ref, added[1 - odd], back)
            give(i - 1)

    def pair(p, carry):
        step(2 * p + 2, 0)
        step(2 * p + 3, 1)
        return carry

    back_pick(1, pick_ref, split, rows[1])
    step(1, 1, sum_last=False)
    lax.fori_loop(0, 3, pair, 0)
    step(8, 0, pick_next=False)
    back_sum(0, sum_ref, added[0], back)


def smooth(angle, slab, c_ref, zlow, zhigh, ylow, yhigh, next_ref):
    lane = lax.broadcasted_iota(jnp.int32, (8, 128), 1)
    sub = lax.broadcasted_iota(jnp.int32, (8, 128), 0)
    has_zlow = (slab > 0).astype(f32)
    has_zhigh = (slab < 63).astype(f32)
    has_ylow = (angle > 0).astype(f32)
    has_yhigh = (angle < 3).astype(f32)

    def one(k, carry):
        c = c_ref[k]
        below, above = ylow[pl.ds(k, 1), :] * has_ylow, yhigh[pl.ds(k, 1), :] * has_yhigh
        half = (c[:, :128], c[:, 128:])
        deep = (zlow[k] * has_zlow + half[1], half[0] + zhigh[k] * has_zhigh)
        for zz in range(2):
            v = half[zz]
            at = slice(zz * 128, zz * 128 + 128)
            near = deep[zz]
            near += jnp.where(sub == 0, jnp.broadcast_to(below[:, at], (8, 128)), pltpu.roll(v, 1, 0))
            near += jnp.where(sub == 7, jnp.broadcast_to(above[:, at], (8, 128)), pltpu.roll(v, 7, 0))
            near += jnp.where(lane == 0, 0.0, pltpu.roll(v, 1, 1)) + jnp.where(lane == 127, 0.0, pltpu.roll(v, 127, 1))
            next_ref[k, :, at] = v - (STEP * SMOOTH) * (6.0 * v - near)
        return carry

    lax.fori_loop(0, 48, one, 0, unroll=4)


def prepare_slots(packs, half, pick_v, pick_p, sum_v, sum_p, shift_b):
    row = lax.broadcasted_iota(jnp.int32, (8, 640), 0)
    lane = lax.broadcasted_iota(jnp.int32, (8, 640), 1)
    spread = ((lane < 256) & (row == 0)) | ((lane >= 256) & (lane < 512) & (row == 1)) | ((lane >= 512) & (row >= 2) & (row <= 4))
    spread = jnp.where(spread, 1.0, 0.0).astype(bf16)
    id_v = lax.rem(lax.broadcasted_iota(jnp.int32, (TS, 192), 1), 64).astype(f32)
    id_p = lax.rem(lax.broadcasted_iota(jnp.int32, (TS, 256), 1), 128).astype(f32)
    sub_v = lax.broadcasted_iota(jnp.int32, (64, TS), 0).astype(f32)
    sub_p = lax.broadcasted_iota(jnp.int32, (128, TS), 0).astype(f32)

    def hit(ids, along):
        return jnp.where(ids == along, 1.0, 0.0).astype(bf16)

    for i in range(8):
        pixel = packs[i, pl.ds(half, 1), :]
        voxel = packs[i, pl.ds(2 + half, 1), :]
        shift = packs[i, pl.ds(4 + half, 1), :]
        split = [part.astype(f32) for part in parts(shift, 3)]
        rows = jnp.concatenate([voxel, pixel] + split + [jnp.zeros((3, 256), f32)], axis=0)
        wide = hot(rows.T.astype(bf16)[:TS], spread)
        at = slice(i * TS, (i + 1) * TS)
        pick_v[at, :] = hit(wide[:, :192], id_v)
        pick_p[at, :] = hit(wide[:, 256:512], id_p)
        shift_b[at, :] = wide[:, 512:640]
        sum_v[i] = hit(voxel[:, :TS], sub_v)
        sum_p[i] = hit(pixel[:, :TS], sub_p)


def prepare_harmonics(harm_all, harm_f, harm_t):
    harm = harm_all[...].reshape(64, 128)

    def spread(rows, columns, along):
        big = lax.broadcasted_iota(jnp.int32, (rows, columns), along)
        small = lax.broadcasted_iota(jnp.int32, (rows, columns), 1 - along)
        return jnp.where(lax.div(big, 8) == small, 1.0, 0.0)

    def diagonal(rows, columns):
        r = lax.broadcasted_iota(jnp.int32, (rows, columns), 0)
        c = lax.broadcasted_iota(jnp.int32, (rows, columns), 1)
        return lax.rem(r, 8) == lax.rem(c, 8)

    wide = dot(harm, spread(128, 384, 1))
    harm_f[...] = jnp.where(diagonal(512, 384), dot(spread(512, 64, 0), wide), 0.0)
    wide = dot(harm.T, spread(64, 512, 1))
    full = jnp.where(diagonal(384, 512), dot(spread(384, 128, 0), wide), 0.0)
    high, low = parts(full, 2)
    harm_t[:, :512] = high
    harm_t[:, 512:1024] = high
    harm_t[:, 1024:] = low


SEM_PACK, SEM_HARM, SEM_FIELD, SEM_SUM, SEM_ALL, SEM_BACK, SEM_HALO, SEM_MIS, SEM_FAR, SEM_NEAR, SEM_PASS = (
    0, 1, 2, 18, 20, 22, 24, 32, 33, 36, 39,
)
SEMS = 42
FAR_FIRST = (4, 3, 5, 2, 6, 1, 7)


def kernel(
    c_hbm, harm_hbm, stretch_hbm, meas_hbm, pix_hbm, vox_hbm, shift_hbm, count_hbm,
    out_ref, mout_ref,
    c_all, harm_v, harm_s, stretch_s, meas_v, pix_v, vox_v, shift_v, count_s,
    pack, packs, blocks, field0, field1, harm_all, harm_f, harm_t, pick_v, pick_p, sum_v, sum_p, shift_b, meas_own,
    c0_ref, c1_ref, next_ref, proj, sums, misfit, rows_a, rows_b, added_a, added_b, total, split, back, got, fields, zlow, zhigh, ylow, yhigh, edges,
    send_sem, recv_sem, load_sem,
):
    angle, x, z, half = position()
    slab = (x * 8 + z) * 2 + half
    mine = x * 2 + half
    block = (angle * 2 + half) * 4 + x
    plane = [
        device(lax.rem(angle + k // 8, 4), lax.rem(x + k // 2, 4), z, lax.rem(half + k % 2, 2)) for k in range(1, 32)
    ]
    line = [device(angle, x, lax.rem(z + k, 8), half) for k in range(1, 8)]
    beyond = (angle, lax.rem(slab + 2 * half + 63, 64))
    partners = plane + line + [beyond]
    above = (angle, lax.rem(slab + 1, 64))
    below = (angle, lax.rem(slab + 63, 64))
    right = (lax.rem(angle + 1, 4), slab)
    left = (lax.rem(angle + 3, 4), slab)
    back_of = [((4 - i // 2) % 4) * 2 + i % 2 for i in range(8)]

    loads = [
        pltpu.make_async_copy(src, dst, load_sem.at[n])
        for n, (src, dst) in enumerate(
            [
                (c_hbm, c_all), (harm_hbm, harm_s), (harm_hbm, harm_v), (pix_hbm, pix_v), (vox_hbm, vox_v),
                (shift_hbm, shift_v), (count_hbm, count_s), (meas_hbm, meas_v), (stretch_hbm, stretch_s),
            ]
        )
    ]
    for load in loads:
        load.start()
    signal(partners)
    for load in loads:
        load.wait()

    pixel = pix_v[...]
    pixel = lax.rem(lax.div(pixel, 4), 8) * 16 + lax.div(pixel, 32) * 4 + lax.rem(pixel, 4)
    first = lax.broadcasted_iota(jnp.int32, (2, TS), 0) == 0
    valid = lax.broadcasted_iota(jnp.int32, (2, TS), 1) < jnp.where(first, count_s[0, 0], count_s[0, 1])
    pack[...] = jnp.zeros_like(pack)
    pack[0:2, :TS] = pixel.astype(f32)
    pack[2:4, :TS] = vox_v[...].astype(f32)
    pack[4:6, :TS] = jnp.where(valid, shift_v[...], FAR)
    pack[8:16] = meas_v[0]
    pack[16:24] = meas_v[1]
    packs[0] = pack[...]
    harm_all[angle] = jnp.zeros((16, 128), f32)
    harm_all[angle, 0:8, 0:45] = harm_v[0]
    harm_all[angle, 8:16, 0:45] = harm_v[1]
    quarter_y = pl.ds(pl.multiple_of(angle * 8, 8), 8)
    c0_ref[:45, :, 0:128] = c_all[:, 0, quarter_y, :]
    c0_ref[:45, :, 128:256] = c_all[:, 1, quarter_y, :]
    c0_ref[45:] = jnp.zeros((3, 8, 256), f32)

    def first_fields(which, segments, dest):
        for s in range(2):
            for zz in range(2):
                total = [None] * 4
                for k in range(45):
                    h = harm_s[which, segments * 2 + s, k]
                    for y in range(4):
                        term = c_all[k, zz, y * 8 : y * 8 + 8, :] * h
                        total[y] = term if k == 0 else total[y] + term
                for y in range(4):
                    dest[y, s, :, zz * 128 : zz * 128 + 128] = total[y]

    def first_block(i, carry):
        first_fields(lax.rem(half + lax.rem(i, 2), 2), lax.rem(x + lax.div(i, 2), 4), blocks.at[i])
        return carry

    lax.fori_loop(0, 8, first_block, 0)
    await_signals(partners)
    peers = [device(angle, lax.rem(x + i // 2, 4), z, lax.rem(half + i % 2, 2)) for i in range(8)]
    for i in range(1, 8):
        send(pack, packs.at[back_of[i]], send_sem.at[SEM_PACK], recv_sem.at[SEM_PACK], peers[i])
    for i in range(1, 8):
        send(
            blocks.at[i], field0.at[back_of[i]], send_sem.at[SEM_FIELD], recv_sem.at[SEM_FIELD + back_of[i]], peers[i]
        )
    for k in range(1, 4):
        target = device(lax.rem(angle + k, 4), x, z, half)
        send(harm_all.at[angle], harm_all.at[angle], send_sem.at[SEM_HARM], recv_sem.at[SEM_HARM], target)

    def halos(it, c_ref):
        at = SEM_HALO + it * 4
        edges[it, 0] = c_ref[:, 7, :]
        edges[it, 1] = c_ref[:, 0, :]
        send(c_ref.at[:, :, pl.ds(128, 128)], zlow.at[it], send_sem.at[at], recv_sem.at[at], above)
        send(c_ref.at[:, :, pl.ds(0, 128)], zhigh.at[it], send_sem.at[at + 1], recv_sem.at[at + 1], below)
        send(edges.at[it, 0], ylow.at[it], send_sem.at[at + 2], recv_sem.at[at + 2], right)
        send(edges.at[it, 1], yhigh.at[it], send_sem.at[at + 3], recv_sem.at[at + 3], left)

    def drain_halos(it, sems):
        for n, ref in enumerate((zlow, zhigh, ylow, yhigh)):
            drain(ref.at[it], sems.at[SEM_HALO + it * 4 + n])

    field0[0] = blocks[0]
    a = stretch_s[half]
    drain(packs.at[pl.ds(0, 7)], recv_sem.at[SEM_PACK])
    prepare_slots(packs, half, pick_v, pick_p, sum_v, sum_p, shift_b)
    for n in range(8):
        i = lax.rem(n // 2 - x + 4, 4) * 2 + lax.rem(n % 2 - half + 2, 2)
        for s in range(2):
            line_of = packs[i, pl.ds(8 + half * 8 + x * 2 + s, 1), :]
            for tile in range(2):
                row = n * 2 + tile
                meas_own[row : row + 1, s * 128 : s * 128 + 128] = line_of[:, tile * 128 : tile * 128 + 128]

    for it in range(2):
        field = field0 if it == 0 else field1
        c_ref = c0_ref if it == 0 else c1_ref
        sem_field = SEM_FIELD + it * 8

        def arrived(i):
            drain(field.at[i], recv_sem.at[sem_field + i])

        project_all(a, shift_b, pick_v, sum_p, field, arrived, (rows_a, rows_b), (added_a, added_b), total)
        proj[it] = total[...].reshape(8, 16, 256)

        for k in FAR_FIRST:
            zz = lax.rem(z + k, 8)
            send(proj.at[it, zz], sums.at[it, k - 1], send_sem.at[SEM_SUM + it], recv_sem.at[SEM_SUM + it], line[k - 1])
        drain(sums.at[it], recv_sem.at[SEM_SUM + it])
        own = proj[it, z] - meas_own[...]
        for k in range(7):
            own = own + sums[it, k]
        misfit[it, z] = own
        for k in FAR_FIRST:
            send(misfit.at[it, z], misfit.at[it, z], send_sem.at[SEM_ALL + it], recv_sem.at[SEM_ALL + it], line[k - 1])
        halos(it, c_ref)
        if it == 0:
            drain(harm_all.at[pl.ds(0, 3)], recv_sem.at[SEM_HARM])
            prepare_harmonics(harm_all, harm_f, harm_t)
        else:
            mout_ref[mine] = own
            for i in range(1, 8):
                send(misfit.at[it, z], mout_ref.at[mine], send_sem.at[SEM_MIS], recv_sem.at[SEM_MIS], peers[i])
        drain(misfit.at[it, pl.ds(0, 7)], recv_sem.at[SEM_ALL + it])

        high, low = parts(misfit[it].reshape(128, 256), 2)
        split[:128] = high
        split[128:] = low

        def give(i):
            xx, hh = lax.rem(x + lax.div(i, 2), 4), lax.rem(half + lax.rem(i, 2), 2)
            for k in range(4):
                aa = lax.rem(angle + k, 4)
                send(
                    back.at[it, i, aa], got.at[it, block],
                    send_sem.at[SEM_BACK + it], recv_sem.at[SEM_BACK + it], device(aa, xx, z, hh),
                )

        back_all(a, shift_b, pick_p, sum_v, split, give, (rows_a, rows_b), (added_a, added_b), back.at[it])
        for k in range(1, 4):
            aa = lax.rem(angle + k, 4)
            send(
                back.at[it, 0, aa], got.at[it, block],
                send_sem.at[SEM_BACK + it], recv_sem.at[SEM_BACK + it], device(aa, x, z, half),
            )
        got[it, block] = back[it, 0, angle]
        drain_halos(it, recv_sem)
        smooth(angle, slab, c_ref, zlow.at[it], zhigh.at[it], ylow.at[it], yhigh.at[it], next_ref)
        drain(got.at[it, pl.ds(0, 31)], recv_sem.at[SEM_BACK + it])
        high, low = parts(got[it].reshape(512, 256), 2)
        terms = jnp.concatenate([high, low, high], axis=0)

        if it == 0:
            new = next_ref[...].reshape(384, 256) - STEP * hot(harm_t[...], terms)
            c1_ref[...] = new.reshape(48, 8, 256)
            fields[...] = dot(harm_f[...], new).reshape(32, 2, 8, 256)
            for k in sorted(range(1, 32), key=lambda k: (k % 8, k)):
                aa, xx, hh = lax.rem(angle + k // 8, 4), lax.rem(x + k % 8 // 2, 4), lax.rem(half + k % 2, 2)
                to = back_of[k % 8]
                send(
                    fields.at[(aa * 2 + hh) * 4 + xx], field1.at[to, angle],
                    send_sem.at[SEM_FIELD + 8], recv_sem.at[SEM_FIELD + 8 + to], device(aa, xx, z, hh),
                )
            field1[0, angle] = fields[block]
            drain(field1.at[0, pl.ds(0, 3)], recv_sem.at[SEM_FIELD + 8])
        else:
            far = lax.rem(angle + 2, 4)
            beside = angle + 1 - 2 * lax.rem(angle, 2)
            groups = ((0, 16), (16, 16), (32, 13))

            def quarter(start, size, which):
                return out_ref.at[pl.ds(start, size), :, pl.ds(pl.multiple_of(which * 8, 8), 8), :]

            for g, (start, size) in enumerate(groups):
                rows = slice(start * 8, (start + 16) * 8)
                new = next_ref[start : start + 16].reshape(128, 256) - STEP * hot(harm_t[rows, :], terms)
                new = new.reshape(16, 8, 256)[:size]
                for zz in range(2):
                    out_ref[start : start + size, zz, quarter_y, :] = new[:, :, zz * 128 : zz * 128 + 128]
                piece = quarter(start, size, angle)
                send(piece, piece, send_sem.at[SEM_FAR + g], recv_sem.at[SEM_FAR + g], (far, slab))
                send(piece, piece, send_sem.at[SEM_NEAR + g], recv_sem.at[SEM_NEAR + g], (beside, slab))
            for g, (start, size) in enumerate(groups):
                piece = quarter(start, size, far)
                drain(piece, recv_sem.at[SEM_FAR + g])
                send(piece, piece, send_sem.at[SEM_PASS + g], recv_sem.at[SEM_PASS + g], (beside, slab))
            for g, (start, size) in enumerate(groups):
                piece = quarter(start, size, angle)
                drain(piece, recv_sem.at[SEM_NEAR + g])
                drain(piece, recv_sem.at[SEM_PASS + g])
                for first in (SEM_FAR, SEM_NEAR, SEM_PASS):
                    drain(piece, send_sem.at[first + g])
            drain(mout_ref.at[pl.ds(0, 7)], recv_sem.at[SEM_MIS])
            drain(mout_ref.at[pl.ds(0, 7)], send_sem.at[SEM_MIS])

    drain(packs.at[pl.ds(0, 7)], send_sem.at[SEM_PACK])
    drain(harm_all.at[pl.ds(0, 3)], send_sem.at[SEM_HARM])
    drain(field0.at[pl.ds(0, 7)], send_sem.at[SEM_FIELD])
    drain(got.at[0, pl.ds(0, 31)], send_sem.at[SEM_FIELD + 8])
    for it in range(2):
        drain(sums.at[it], send_sem.at[SEM_SUM + it])
        drain(misfit.at[it, pl.ds(0, 7)], send_sem.at[SEM_ALL + it])
        drain(got.at[it, pl.ds(0, 31)], send_sem.at[SEM_BACK + it])
        drain_halos(it, send_sem)


def per_device(coefficients, harmonics, stretch, measured, tile_pixel, tile_voxel, tile_shift, tile_count):
    angle, x, z, half = position()
    operands = (coefficients, harmonics, stretch, measured, tile_pixel, tile_voxel, tile_shift, tile_count.T)
    scratch = [
        pltpu.VMEM((45, 2, 32, 128), f32),
        pltpu.VMEM((2, 8, 45), f32),
        pltpu.SMEM((2, 8, 45), f32),
        pltpu.SMEM((2,), f32),
        pltpu.VMEM((2, 8, 256), f32),
        pltpu.VMEM((2, TS), jnp.int32),
        pltpu.VMEM((2, TS), jnp.int32),
        pltpu.VMEM((2, TS), f32),
        pltpu.SMEM((1, 2), jnp.int32),
        pltpu.VMEM((24, 256), f32),
        pltpu.VMEM((8, 24, 256), f32),
        pltpu.VMEM((8, 4, 2, 8, 256), f32),
        pltpu.VMEM((8, 4, 2, 8, 256), f32),
        pltpu.VMEM((8, 4, 2, 8, 256), f32),
        pltpu.VMEM((4, 16, 128), f32),
        pltpu.VMEM((512, 384), f32),
        pltpu.VMEM((384, 1536), bf16),
        pltpu.VMEM((8 * TS, 192), bf16),
        pltpu.VMEM((8 * TS, 256), bf16),
        pltpu.VMEM((8, 64, TS), bf16),
        pltpu.VMEM((8, 128, TS), bf16),
        pltpu.VMEM((8 * TS, 128), f32),
        pltpu.VMEM((16, 256), f32),
        pltpu.VMEM((48, 8, 256), f32),
        pltpu.VMEM((48, 8, 256), f32),
        pltpu.VMEM((48, 8, 256), f32),
        pltpu.VMEM((2, 8, 16, 256), f32),
        pltpu.VMEM((2, 7, 16, 256), f32),
        pltpu.VMEM((2, 8, 16, 256), f32),
        pltpu.VMEM((TS, 512), f32),
        pltpu.VMEM((TS, 512), f32),
        pltpu.VMEM((TS, 256), f32),
        pltpu.VMEM((TS, 256), f32),
        pltpu.VMEM((128, 256), f32),
        pltpu.VMEM((256, 256), bf16),
        pltpu.VMEM((2, 8, 4, 2, 8, 256), f32),
        pltpu.VMEM((2, 32, 2, 8, 256), f32),
        pltpu.VMEM((32, 2, 8, 256), f32),
        pltpu.VMEM((2, 48, 8, 128), f32),
        pltpu.VMEM((2, 48, 8, 128), f32),
        pltpu.VMEM((2, 48, 256), f32),
        pltpu.VMEM((2, 48, 256), f32),
        pltpu.VMEM((2, 2, 48, 256), f32),
        pltpu.SemaphoreType.DMA((SEMS,)),
        pltpu.SemaphoreType.DMA((SEMS,)),
        pltpu.SemaphoreType.DMA((9,)),
    ]
    updated, mout = pl.pallas_call(
        kernel,
        out_shape=(jax.ShapeDtypeStruct((45, 2, 32, 128), f32), jax.ShapeDtypeStruct((8, 16, 256), f32)),
        in_specs=[pl.BlockSpec(memory_space=pltpu.HBM)] * 8,
        out_specs=(VM, VM),
        scratch_shapes=scratch,
        compiler_params=pltpu.CompilerParams(collective_id=0, has_side_effects=True, vmem_limit_bytes=LIMIT),
        name="tomography",
    )(*operands)
    mout = lax.dynamic_index_in_dim(mout.reshape(4, 2, 8, 2, 2, 128), x * 2 + half, 2, keepdims=False)
    misfit = mout.transpose(1, 0, 3, 2, 4).reshape(2, 8, 256)
    return updated, misfit


def solution(mesh):
    in_specs = (
        P(None, "slab", None, None),
        P("angle", None, None),
        P("angle"),
        P("angle", None, "slab"),
        P("angle", "slab"),
        P("angle", "slab"),
        P("angle", "slab"),
        P("angle", "slab"),
    )
    out_specs = (P(None, "slab", None, None), P("angle", None, "slab"))
    return jax.shard_map(per_device, mesh=mesh, in_specs=in_specs, out_specs=out_specs, check_vma=False)
```

```python
import jax
import jax.numpy as jnp
from jax import lax
from jax.experimental import pallas as pl
from jax.experimental.pallas import tpu as pltpu
from jax.sharding import PartitionSpec as P

f32 = jnp.float32
bf16 = jnp.bfloat16
MESH = pl.DeviceIdType.MESH
STEP = 0.003
SMOOTH = 6.0
FAR = 128.0
FIX = 23
TS = 192
CHUNK = 48
TAKE = lax.GatherDimensionNumbers(
    offset_dims=(), collapsed_slice_dims=(1,), start_index_map=(1,), operand_batching_dims=(0,), start_indices_batching_dims=(0,)
)

VM = pl.BlockSpec(memory_space=pltpu.VMEM)
SM = pl.BlockSpec(memory_space=pltpu.SMEM)
LIMIT = 56 * 2**20


def position():
    angle = lax.axis_index("angle")
    slab = lax.axis_index("slab")
    return angle, lax.div(slab, 16), lax.rem(lax.div(slab, 2), 8), lax.rem(slab, 2)


def device(angle, x, z, half):
    return (angle, (x * 8 + z) * 2 + half)


def signal(partners):
    barrier = pltpu.get_barrier_semaphore()
    for partner in partners:
        pl.semaphore_signal(barrier, inc=1, device_id=partner, device_id_type=MESH)


def await_signals(partners):
    pl.semaphore_wait(pltpu.get_barrier_semaphore(), len(partners))


def send(src, dst, send_sem, recv_sem, target):
    pltpu.make_async_remote_copy(
        src_ref=src, dst_ref=dst, send_sem=send_sem, recv_sem=recv_sem, device_id=target, device_id_type=MESH
    ).start()


def drain(like, sem):
    pltpu.make_async_copy(like, like, sem).wait()


def dot(a, b):
    return jnp.dot(a, b, preferred_element_type=f32, precision=lax.Precision.HIGHEST)


def hot(a, b):
    return jnp.dot(a, b, preferred_element_type=f32)


def parts(value, count):
    found = []
    for _ in range(count - 1):
        part = value.astype(bf16)
        found.append(part)
        value = value - part.astype(f32)
    return found + [value.astype(bf16)]


def take(values, lanes):
    return lax.gather(values, lanes[..., None], TAKE, slice_sizes=(1, 1), mode=lax.GatherScatterMode.PROMISE_IN_BOUNDS)


def project_pick(i, pick_ref, field, picked):
    rows = [
        jnp.concatenate([field[i, y, s, :, zz * 128 : zz * 128 + 128] for s in range(2)], axis=1)
        for zz in range(2)
        for y in range(4)
    ]
    rows = jnp.concatenate(rows, axis=0)
    ahead = [pltpu.roll(rows[:, s * 128 : s * 128 + 128], 127, 1) for s in range(2)]
    split = jnp.concatenate(parts(jnp.concatenate([rows] + ahead, axis=1), 3), axis=0)
    picked[...] = hot(pick_ref[slice(i * TS, (i + 1) * TS), :], split)


def project_slots(i, stretch, shift_ref, picked, contrib):
    one = 1 << FIX
    scale = 1.0 / one
    lane = lax.broadcasted_iota(jnp.int32, (1, 128), 1)
    step = (jnp.full((1, 128), stretch, f32) * one + 0.5).astype(jnp.int32)
    inverse = 1.0 / step.astype(f32)
    steps = step * lane

    def first_of(distance):
        first = jnp.ceil(distance.astype(f32) * inverse - 2.0e-4).astype(jnp.int32)
        first = jnp.where(first * step < distance, first + 1, first)
        return jnp.maximum(first, 0)

    for c in range(TS // CHUNK):
        at = slice(c * CHUNK, (c + 1) * CHUNK)
        start = (shift_ref[slice(i * TS + c * CHUNK, i * TS + (c + 1) * CHUNK), :] * one + 0.5).astype(jnp.int32)
        here = start + steps
        after = here + step
        w1 = (here & (one - 1)).astype(f32) * scale
        w0 = 1.0 - w1
        both = (lax.shift_right_arithmetic(here, FIX) == lax.shift_right_arithmetic(after, FIX)) & (lane < 127)
        next1 = (after & (one - 1)).astype(f32) * scale
        next0 = jnp.where(both, 1.0 - next1, 0.0)
        next1 = jnp.where(both, next1, 0.0)
        distance = (lane << FIX) - start
        first0, first1 = first_of(distance), first_of(distance - one)
        has0 = (first0 <= 127) & (distance > -one)
        has1 = (first1 <= 127) & (distance > 0)
        first0, first1 = first0 & 127, first1 & 127
        for s in range(2):
            f = picked[at, s * 128 : s * 128 + 128]
            g = picked[at, 256 + s * 128 : 256 + s * 128 + 128]
            low = jnp.where(has0, take(w0 * f + next0 * g, first0), 0.0)
            high = jnp.where(has1, take(w1 * f + next1 * g, first1), 0.0)
            contrib[at, s * 128 : s * 128 + 128] = low + high


def project_sum(i, sum_ref, contrib, total):
    for part in parts(contrib[...], 3):
        total[...] += hot(sum_ref[i], part)


def project_all(stretch, shift_ref, pick_ref, sum_ref, field, arrived, rows, added, total):
    total[...] = jnp.zeros_like(total)

    def step(n, odd):
        if n < 7:
            arrived(ARRIVE[n + 1])
            project_pick(ARRIVE[n + 1], pick_ref, field, rows[1 - odd])
        project_slots(ARRIVE[n], stretch, shift_ref, rows[odd], added[odd])
        if n > 0:
            project_sum(ARRIVE[n - 1], sum_ref, added[1 - odd], total)

    project_pick(ARRIVE[0], pick_ref, field, rows[0])
    for n in range(8):
        step(n, n % 2)
    project_sum(ARRIVE[7], sum_ref, added[1], total)


def back_pick(i, pick_ref, split, picked):
    picked[:, :256] = hot(pick_ref[slice(i * TS, (i + 1) * TS), :], split[...])


def back_slots(i, stretch, shift_ref, picked, contrib):
    lane = lax.broadcasted_iota(jnp.int32, (1, 128), 1).astype(f32) * stretch
    for c in range(TS // CHUNK):
        at = slice(c * CHUNK, (c + 1) * CHUNK)
        t = shift_ref[slice(i * TS + c * CHUNK, i * TS + (c + 1) * CHUNK), :] + lane
        p0 = jnp.floor(t)
        w1 = t - p0
        w0 = jnp.where(p0 <= 127.0, 1.0 - w1, 0.0)
        w1 = jnp.where(p0 <= 126.0, w1, 0.0)
        first = p0.astype(jnp.int32)
        lane0, lane1 = first & 127, (first + 1) & 127
        for s in range(2):
            m = picked[at, s * 128 : s * 128 + 128]
            contrib[at, s * 128 : s * 128 + 128] = take(m, lane0) * w0 + take(m, lane1) * w1


def back_sum(i, sum_ref, contrib, back):
    high, low = parts(contrib[...], 2)
    total = hot(sum_ref[i], high) + hot(sum_ref[i], low)
    for y in range(4):
        for s in range(2):
            for zz in range(2):
                row = zz * 32 + y * 8
                back[i, y, s, :, zz * 128 : zz * 128 + 128] = total[row : row + 8, s * 128 : s * 128 + 128]


def back_all(stretch, shift_ref, pick_ref, sum_ref, split, give, rows, added, back):
    back_pick(DEPART[0], pick_ref, split, rows[0])
    for n in range(8):
        odd = n % 2
        if n < 7:
            back_pick(DEPART[n + 1], pick_ref, split, rows[1 - odd])
        back_slots(DEPART[n], stretch, shift_ref, rows[odd], added[odd])
        if n > 0:
            back_sum(DEPART[n - 1], sum_ref, added[1 - odd], back)
            give(DEPART[n - 1])
    back_sum(DEPART[7], sum_ref, added[1], back)


def smooth(angle, slab, c_ref, zlow, zhigh, ylow, yhigh, next_ref):
    lane = lax.broadcasted_iota(jnp.int32, (8, 128), 1)
    sub = lax.broadcasted_iota(jnp.int32, (8, 128), 0)
    has_zlow = (slab > 0).astype(f32)
    has_zhigh = (slab < 63).astype(f32)
    has_ylow = (angle > 0).astype(f32)
    has_yhigh = (angle < 3).astype(f32)

    def one(k, carry):
        c = c_ref[k]
        below, above = ylow[pl.ds(k, 1), :] * has_ylow, yhigh[pl.ds(k, 1), :] * has_yhigh
        half = (c[:, :128], c[:, 128:])
        deep = (zlow[k] * has_zlow + half[1], half[0] + zhigh[k] * has_zhigh)
        for zz in range(2):
            v = half[zz]
            at = slice(zz * 128, zz * 128 + 128)
            near = deep[zz]
            near += jnp.where(sub == 0, jnp.broadcast_to(below[:, at], (8, 128)), pltpu.roll(v, 1, 0))
            near += jnp.where(sub == 7, jnp.broadcast_to(above[:, at], (8, 128)), pltpu.roll(v, 7, 0))
            near += jnp.where(lane == 0, 0.0, pltpu.roll(v, 1, 1)) + jnp.where(lane == 127, 0.0, pltpu.roll(v, 127, 1))
            next_ref[k, :, at] = v - (STEP * SMOOTH) * (6.0 * v - near)
        return carry

    lax.fori_loop(0, 48, one, 0, unroll=4)


def prepare_slots(packs, half, pick_v, pick_p, sum_v, sum_p, shift_b):
    row = lax.broadcasted_iota(jnp.int32, (8, 640), 0)
    lane = lax.broadcasted_iota(jnp.int32, (8, 640), 1)
    spread = ((lane < 256) & (row == 0)) | ((lane >= 256) & (lane < 512) & (row == 1)) | ((lane >= 512) & (row >= 2) & (row <= 4))
    spread = jnp.where(spread, 1.0, 0.0).astype(bf16)
    id_v = lax.rem(lax.broadcasted_iota(jnp.int32, (TS, 192), 1), 64).astype(f32)
    id_p = lax.rem(lax.broadcasted_iota(jnp.int32, (TS, 256), 1), 128).astype(f32)
    sub_v = lax.broadcasted_iota(jnp.int32, (64, TS), 0).astype(f32)
    sub_p = lax.broadcasted_iota(jnp.int32, (128, TS), 0).astype(f32)

    def hit(ids, along):
        return jnp.where(ids == along, 1.0, 0.0).astype(bf16)

    for i in range(8):
        pixel = packs[i, pl.ds(half, 1), :]
        voxel = packs[i, pl.ds(2 + half, 1), :]
        shift = packs[i, pl.ds(4 + half, 1), :]
        split = [part.astype(f32) for part in parts(shift, 3)]
        rows = jnp.concatenate([voxel, pixel] + split + [jnp.zeros((3, 256), f32)], axis=0)
        wide = hot(rows.T.astype(bf16)[:TS], spread)
        at = slice(i * TS, (i + 1) * TS)
        pick_v[at, :] = hit(wide[:, :192], id_v)
        pick_p[at, :] = hit(wide[:, 256:512], id_p)
        shift_b[at, :] = wide[:, 512:640]
        sum_v[i] = hit(voxel[:, :TS], sub_v)
        sum_p[i] = hit(pixel[:, :TS], sub_p)


def prepare_harmonics(harm_all, harm_f, harm_t):
    harm = harm_all[...].reshape(64, 128)

    def spread(rows, columns, along):
        big = lax.broadcasted_iota(jnp.int32, (rows, columns), along)
        small = lax.broadcasted_iota(jnp.int32, (rows, columns), 1 - along)
        return jnp.where(lax.div(big, 8) == small, 1.0, 0.0)

    def diagonal(rows, columns):
        r = lax.broadcasted_iota(jnp.int32, (rows, columns), 0)
        c = lax.broadcasted_iota(jnp.int32, (rows, columns), 1)
        return lax.rem(r, 8) == lax.rem(c, 8)

    wide = dot(harm, spread(128, 384, 1))
    harm_f[...] = jnp.where(diagonal(512, 384), dot(spread(512, 64, 0), wide), 0.0)
    wide = dot(harm.T, spread(64, 512, 1))
    full = jnp.where(diagonal(384, 512), dot(spread(384, 128, 0), wide), 0.0)
    high, low = parts(full, 2)
    harm_t[:, :512] = high
    harm_t[:, 512:1024] = high
    harm_t[:, 1024:] = low


SEM_PACK, SEM_HARM, SEM_FIELD, SEM_SUM, SEM_ALL, SEM_BACK, SEM_HALO, SEM_MIS, SEM_FAR, SEM_NEAR, SEM_PASS = (
    0, 1, 2, 18, 20, 22, 24, 32, 33, 37, 41,
)
SEMS = 45
FAR_FIRST = (4, 3, 5, 2, 6, 1, 7)
ARRIVE = (0, 5, 3, 7, 4, 1, 2, 6)
DEPART = (5, 3, 7, 4, 1, 2, 6, 0)


def kernel(
    c_hbm, harm_hbm, stretch_hbm, meas_hbm, pix_hbm, vox_hbm, shift_hbm, count_hbm,
    out_ref, mis_ref,
    c_all, harm_v, harm_s, stretch_s, meas_v, pix_v, vox_v, shift_v, count_s,
    pack, packs, blocks, field0, field1, harm_all, harm_f, harm_t, pick_v, pick_p, sum_v, sum_p, shift_b, meas_own,
    c0_ref, c1_ref, next_ref, proj, sums, misfit, rows_a, rows_b, added_a, added_b, total, split, back, got, fields, deep, ylow, yhigh, edges, mine_out, mine_got,
    send_sem, recv_sem, load_sem,
):
    angle, x, z, half = position()
    slab = (x * 8 + z) * 2 + half
    mine = x * 2 + half
    block = (angle * 2 + half) * 4 + x
    plane = [
        device(lax.rem(angle + k // 8, 4), lax.rem(x + k // 2, 4), z, lax.rem(half + k % 2, 2)) for k in range(1, 32)
    ]
    line = [device(angle, x, lax.rem(z + k, 8), half) for k in range(1, 8)]
    beyond = (angle, lax.rem(slab + 2 * half + 63, 64))
    partners = plane + line + [beyond]
    right = (lax.rem(angle + 1, 4), slab)
    left = (lax.rem(angle + 3, 4), slab)
    back_of = [((4 - i // 2) % 4) * 2 + i % 2 for i in range(8)]

    loads = [
        pltpu.make_async_copy(src, dst, load_sem.at[n])
        for n, (src, dst) in enumerate(
            [
                (c_hbm, c_all), (harm_hbm, harm_s), (harm_hbm, harm_v), (pix_hbm, pix_v), (vox_hbm, vox_v),
                (shift_hbm, shift_v), (count_hbm, count_s), (meas_hbm, meas_v), (stretch_hbm, stretch_s),
            ]
        )
    ]
    for load in loads:
        load.start()
    signal(partners)
    for load in loads[1:]:
        load.wait()

    pixel = pix_v[...]
    pixel = lax.rem(lax.div(pixel, 4), 8) * 16 + lax.div(pixel, 32) * 4 + lax.rem(pixel, 4)
    first = lax.broadcasted_iota(jnp.int32, (2, TS), 0) == 0
    valid = lax.broadcasted_iota(jnp.int32, (2, TS), 1) < jnp.where(first, count_s[0, 0], count_s[0, 1])
    pack[...] = jnp.zeros_like(pack)
    pack[0:2, :TS] = pixel.astype(f32)
    pack[2:4, :TS] = vox_v[...].astype(f32)
    pack[4:6, :TS] = jnp.where(valid, shift_v[...], FAR)
    pack[8:16] = meas_v[0]
    pack[16:24] = meas_v[1]
    packs[0] = pack[...]
    harm_all[angle] = jnp.zeros((16, 128), f32)
    harm_all[angle, 0:8, 0:45] = harm_v[0]
    harm_all[angle, 8:16, 0:45] = harm_v[1]
    quarter_y = pl.ds(pl.multiple_of(angle * 8, 8), 8)
    await_signals(partners)
    peers = [device(angle, lax.rem(x + i // 2, 4), z, lax.rem(half + i % 2, 2)) for i in range(8)]
    for i in range(1, 8):
        send(pack, packs.at[back_of[i]], send_sem.at[SEM_PACK], recv_sem.at[SEM_PACK], peers[i])
    for k in range(1, 4):
        target = device(lax.rem(angle + k, 4), x, z, half)
        send(harm_all.at[angle], harm_all.at[angle], send_sem.at[SEM_HARM], recv_sem.at[SEM_HARM], target)
    loads[0].wait()

    def first_fields(which, segments, dest):
        for s in range(2):
            for zz in range(2):
                total = [None] * 4
                for k in range(45):
                    h = harm_s[which, segments * 2 + s, k]
                    for y in range(4):
                        term = c_all[k, zz, y * 8 : y * 8 + 8, :] * h
                        total[y] = term if k == 0 else total[y] + term
                for y in range(4):
                    dest[y, s, :, zz * 128 : zz * 128 + 128] = total[y]

    for i in DEPART:
        first_fields(lax.rem(half + i % 2, 2), lax.rem(x + i // 2, 4), blocks.at[i])
        if i > 0:
            send(
                blocks.at[i], field0.at[back_of[i]], send_sem.at[SEM_FIELD], recv_sem.at[SEM_FIELD + back_of[i]], peers[i]
            )
    field0[0] = blocks[0]
    c0_ref[:45, :, 0:128] = c_all[:, 0, quarter_y, :]
    c0_ref[:45, :, 128:256] = c_all[:, 1, quarter_y, :]
    c0_ref[45:] = jnp.zeros((3, 8, 256), f32)

    def halos_beside(it, c_ref):
        at = SEM_HALO + it * 4
        edges[it, 0] = c_ref[:, 7, :]
        edges[it, 1] = c_ref[:, 0, :]
        src = c_ref.at[:, :, pl.ds(pl.multiple_of((1 - half) * 128, 128), 128)]
        send(src, deep.at[it, half], send_sem.at[at], recv_sem.at[at], device(angle, x, z, 1 - half))
        send(edges.at[it, 0], ylow.at[it], send_sem.at[at + 2], recv_sem.at[at + 2], right)
        send(edges.at[it, 1], yhigh.at[it], send_sem.at[at + 3], recv_sem.at[at + 3], left)

    def halos_beyond(it, c_ref):
        at = SEM_HALO + it * 4 + 1
        src = c_ref.at[:, :, pl.ds(pl.multiple_of(half * 128, 128), 128)]
        send(src, deep.at[it, 1 - half], send_sem.at[at], recv_sem.at[at], beyond)

    def drain_halos(it, sems):
        for n, ref in enumerate((deep.at[it, 0], deep.at[it, 1], ylow.at[it], yhigh.at[it])):
            drain(ref, sems.at[SEM_HALO + it * 4 + n])

    a = stretch_s[half]
    drain(packs.at[pl.ds(0, 7)], recv_sem.at[SEM_PACK])
    prepare_slots(packs, half, pick_v, pick_p, sum_v, sum_p, shift_b)
    for n in range(8):
        i = lax.rem(n // 2 - x + 4, 4) * 2 + lax.rem(n % 2 - half + 2, 2)
        for s in range(2):
            line_of = packs[i, pl.ds(8 + half * 8 + x * 2 + s, 1), :]
            for tile in range(2):
                row = n * 2 + tile
                meas_own[row : row + 1, s * 128 : s * 128 + 128] = line_of[:, tile * 128 : tile * 128 + 128]

    for it in range(2):
        field = field0 if it == 0 else field1
        c_ref = c0_ref if it == 0 else c1_ref
        sem_field = SEM_FIELD + it * 8

        def arrived(i):
            drain(field.at[i], recv_sem.at[sem_field + i])

        project_all(a, shift_b, pick_v, sum_p, field, arrived, (rows_a, rows_b), (added_a, added_b), total)
        proj[it] = total[...].reshape(8, 16, 256)

        for k in FAR_FIRST:
            zz = lax.rem(z + k, 8)
            send(proj.at[it, zz], sums.at[it, k - 1], send_sem.at[SEM_SUM + it], recv_sem.at[SEM_SUM + it], line[k - 1])
        halos_beside(it, c_ref)
        drain(sums.at[it], recv_sem.at[SEM_SUM + it])
        own = proj[it, z] - meas_own[...]
        for k in range(7):
            own = own + sums[it, k]
        misfit[it, z] = own
        for k in FAR_FIRST:
            send(misfit.at[it, z], misfit.at[it, z], send_sem.at[SEM_ALL + it], recv_sem.at[SEM_ALL + it], line[k - 1])
        halos_beyond(it, c_ref)
        if it == 0:
            drain(harm_all.at[pl.ds(0, 3)], recv_sem.at[SEM_HARM])
            prepare_harmonics(harm_all, harm_f, harm_t)
        else:
            mine_out[...] = jnp.zeros_like(mine_out)
            for n in range(8):
                mine_out[n, 0:2] = own[2 * n : 2 * n + 2]
            for i in range(1, 8):
                there = lax.rem(x + i // 2, 4) * 2 + lax.rem(half + i % 2, 2)
                send(mine_out.at[there], mine_got.at[mine], send_sem.at[SEM_MIS], recv_sem.at[SEM_MIS], peers[i])
            mine_got[mine] = mine_out[mine]
        drain(misfit.at[it, pl.ds(0, 7)], recv_sem.at[SEM_ALL + it])

        high, low = parts(misfit[it].reshape(128, 256), 2)
        split[:128] = high
        split[128:] = low

        def give(i):
            xx, hh = lax.rem(x + i // 2, 4), lax.rem(half + i % 2, 2)
            for k in range(4):
                aa = lax.rem(angle + k, 4)
                send(
                    back.at[it, i, aa], got.at[it, block],
                    send_sem.at[SEM_BACK + it], recv_sem.at[SEM_BACK + it], device(aa, xx, z, hh),
                )

        back_all(a, shift_b, pick_p, sum_v, split, give, (rows_a, rows_b), (added_a, added_b), back.at[it])
        for k in range(1, 4):
            aa = lax.rem(angle + k, 4)
            send(
                back.at[it, 0, aa], got.at[it, block],
                send_sem.at[SEM_BACK + it], recv_sem.at[SEM_BACK + it], device(aa, x, z, half),
            )
        got[it, block] = back[it, 0, angle]
        drain_halos(it, recv_sem)
        smooth(angle, slab, c_ref, deep.at[it, 0], deep.at[it, 1], ylow.at[it], yhigh.at[it], next_ref)
        drain(got.at[it, pl.ds(0, 31)], recv_sem.at[SEM_BACK + it])
        high, low = parts(got[it].reshape(512, 256), 2)
        terms = jnp.concatenate([high, low, high], axis=0)

        if it == 0:
            new = next_ref[...].reshape(384, 256) - STEP * hot(harm_t[...], terms)
            c1_ref[...] = new.reshape(48, 8, 256)
            fields[...] = dot(harm_f[...], new).reshape(32, 2, 8, 256)
            for k in sorted(range(1, 32), key=lambda k: ARRIVE.index(k % 8)):
                aa, xx, hh = lax.rem(angle + k // 8, 4), lax.rem(x + k % 8 // 2, 4), lax.rem(half + k % 2, 2)
                to = back_of[k % 8]
                send(
                    fields.at[(aa * 2 + hh) * 4 + xx], field1.at[to, angle],
                    send_sem.at[SEM_FIELD + 8], recv_sem.at[SEM_FIELD + 8 + to], device(aa, xx, z, hh),
                )
            field1[0, angle] = fields[block]
            drain(field1.at[0, pl.ds(0, 3)], recv_sem.at[SEM_FIELD + 8])
        else:
            far = lax.rem(angle + 2, 4)
            beside = angle + 1 - 2 * lax.rem(angle, 2)
            groups = ((0, 16), (16, 16), (32, 8), (40, 5))

            def quarter(start, size, which):
                return out_ref.at[pl.ds(start, size), :, pl.ds(pl.multiple_of(which * 8, 8), 8), :]

            for g, (start, size) in enumerate(groups):
                span = 16 if start < 32 else 8
                rows = slice(start * 8, (start + span) * 8)
                new = next_ref[start : start + span].reshape(span * 8, 256) - STEP * hot(harm_t[rows, :], terms)
                new = new.reshape(span, 8, 256)[:size]
                for zz in range(2):
                    out_ref[start : start + size, zz, quarter_y, :] = new[:, :, zz * 128 : zz * 128 + 128]
                piece = quarter(start, size, angle)
                send(piece, piece, send_sem.at[SEM_FAR + g], recv_sem.at[SEM_FAR + g], (far, slab))
                send(piece, piece, send_sem.at[SEM_NEAR + g], recv_sem.at[SEM_NEAR + g], (beside, slab))
            for g, (start, size) in enumerate(groups):
                piece = quarter(start, size, far)
                drain(piece, recv_sem.at[SEM_FAR + g])
                send(piece, piece, send_sem.at[SEM_PASS + g], recv_sem.at[SEM_PASS + g], (beside, slab))
            for g, (start, size) in enumerate(groups):
                piece = quarter(start, size, angle)
                drain(piece, recv_sem.at[SEM_NEAR + g])
                drain(piece, recv_sem.at[SEM_PASS + g])
                for first in (SEM_FAR, SEM_NEAR, SEM_PASS):
                    drain(piece, send_sem.at[first + g])
            drain(mine_got.at[pl.ds(0, 7)], recv_sem.at[SEM_MIS])
            drain(mine_out.at[pl.ds(0, 7)], send_sem.at[SEM_MIS])
            for n in range(8):
                for s in range(2):
                    for tile in range(2):
                        row = n // 2 * 2 + s
                        mis_ref[n % 2, row : row + 1, tile * 128 : tile * 128 + 128] = mine_got[
                            n, tile : tile + 1, s * 128 : s * 128 + 128
                        ]

    drain(packs.at[pl.ds(0, 7)], send_sem.at[SEM_PACK])
    drain(harm_all.at[pl.ds(0, 3)], send_sem.at[SEM_HARM])
    drain(field0.at[pl.ds(0, 7)], send_sem.at[SEM_FIELD])
    drain(got.at[0, pl.ds(0, 31)], send_sem.at[SEM_FIELD + 8])
    for it in range(2):
        drain(sums.at[it], send_sem.at[SEM_SUM + it])
        drain(misfit.at[it, pl.ds(0, 7)], send_sem.at[SEM_ALL + it])
        drain(got.at[it, pl.ds(0, 31)], send_sem.at[SEM_BACK + it])
        drain_halos(it, send_sem)


def place_kernel(updated, misfit, updated_out, misfit_out, held, held_misfit, sem_in, sem_out):
    pieces = [(updated.at[pl.ds(n * 5, 5)], held.at[pl.ds(n * 5, 5)], updated_out.at[pl.ds(n * 5, 5)]) for n in range(9)]
    pieces.append((misfit, held_misfit, misfit_out))
    into = [pltpu.make_async_copy(src, mid, sem_in.at[n]) for n, (src, mid, _) in enumerate(pieces)]
    out = [pltpu.make_async_copy(mid, dst, sem_out.at[n]) for n, (_, mid, dst) in enumerate(pieces)]
    for copy in into:
        copy.start()
    for first, second in zip(into, out):
        first.wait()
        second.start()
    for copy in out:
        copy.wait()


def place(updated, misfit):
    return pl.pallas_call(
        place_kernel,
        out_shape=(jax.ShapeDtypeStruct(updated.shape, f32), jax.ShapeDtypeStruct(misfit.shape, f32)),
        in_specs=[pl.BlockSpec(memory_space=pltpu.HBM)] * 2,
        out_specs=(pl.BlockSpec(memory_space=pltpu.HBM),) * 2,
        scratch_shapes=[
            pltpu.VMEM(updated.shape, f32),
            pltpu.VMEM(misfit.shape, f32),
            pltpu.SemaphoreType.DMA((10,)),
            pltpu.SemaphoreType.DMA((10,)),
        ],
        compiler_params=pltpu.CompilerParams(vmem_limit_bytes=LIMIT),
        name="place",
    )(updated, misfit)


def per_device(coefficients, harmonics, stretch, measured, tile_pixel, tile_voxel, tile_shift, tile_count):
    operands = (coefficients, harmonics, stretch, measured, tile_pixel, tile_voxel, tile_shift, tile_count.T)
    scratch = [
        pltpu.VMEM((45, 2, 32, 128), f32),
        pltpu.VMEM((2, 8, 45), f32),
        pltpu.SMEM((2, 8, 45), f32),
        pltpu.SMEM((2,), f32),
        pltpu.VMEM((2, 8, 256), f32),
        pltpu.VMEM((2, TS), jnp.int32),
        pltpu.VMEM((2, TS), jnp.int32),
        pltpu.VMEM((2, TS), f32),
        pltpu.SMEM((1, 2), jnp.int32),
        pltpu.VMEM((24, 256), f32),
        pltpu.VMEM((8, 24, 256), f32),
        pltpu.VMEM((8, 4, 2, 8, 256), f32),
        pltpu.VMEM((8, 4, 2, 8, 256), f32),
        pltpu.VMEM((8, 4, 2, 8, 256), f32),
        pltpu.VMEM((4, 16, 128), f32),
        pltpu.VMEM((512, 384), f32),
        pltpu.VMEM((384, 1536), bf16),
        pltpu.VMEM((8 * TS, 192), bf16),
        pltpu.VMEM((8 * TS, 256), bf16),
        pltpu.VMEM((8, 64, TS), bf16),
        pltpu.VMEM((8, 128, TS), bf16),
        pltpu.VMEM((8 * TS, 128), f32),
        pltpu.VMEM((16, 256), f32),
        pltpu.VMEM((48, 8, 256), f32),
        pltpu.VMEM((48, 8, 256), f32),
        pltpu.VMEM((48, 8, 256), f32),
        pltpu.VMEM((2, 8, 16, 256), f32),
        pltpu.VMEM((2, 7, 16, 256), f32),
        pltpu.VMEM((2, 8, 16, 256), f32),
        pltpu.VMEM((TS, 512), f32),
        pltpu.VMEM((TS, 512), f32),
        pltpu.VMEM((TS, 256), f32),
        pltpu.VMEM((TS, 256), f32),
        pltpu.VMEM((128, 256), f32),
        pltpu.VMEM((256, 256), bf16),
        pltpu.VMEM((2, 8, 4, 2, 8, 256), f32),
        pltpu.VMEM((2, 32, 2, 8, 256), f32),
        pltpu.VMEM((32, 2, 8, 256), f32),
        pltpu.VMEM((2, 2, 48, 8, 128), f32),
        pltpu.VMEM((2, 48, 256), f32),
        pltpu.VMEM((2, 48, 256), f32),
        pltpu.VMEM((2, 2, 48, 256), f32),
        pltpu.VMEM((8, 8, 256), f32),
        pltpu.VMEM((8, 8, 256), f32),
        pltpu.SemaphoreType.DMA((SEMS,)),
        pltpu.SemaphoreType.DMA((SEMS,)),
        pltpu.SemaphoreType.DMA((9,)),
    ]
    updated, misfit = pl.pallas_call(
        kernel,
        out_shape=(jax.ShapeDtypeStruct((45, 2, 32, 128), f32), jax.ShapeDtypeStruct((2, 8, 256), f32)),
        in_specs=[pl.BlockSpec(memory_space=pltpu.HBM)] * 8,
        out_specs=(VM, VM),
        scratch_shapes=scratch,
        compiler_params=pltpu.CompilerParams(collective_id=0, has_side_effects=True, vmem_limit_bytes=LIMIT),
        name="tomography",
    )(*operands)
    return place(updated, misfit)


def solution(mesh):
    in_specs = (
        P(None, "slab", None, None),
        P("angle", None, None),
        P("angle"),
        P("angle", None, "slab"),
        P("angle", "slab"),
        P("angle", "slab"),
        P("angle", "slab"),
        P("angle", "slab"),
    )
    out_specs = (P(None, "slab", None, None), P("angle", None, "slab"))
    return jax.shard_map(per_device, mesh=mesh, in_specs=in_specs, out_specs=out_specs, check_vma=False)
```
